512 devices in a mesh: tm: 8 (over z), space: 64 (over x, y, core).
Axes of the slice: x: 4, y: 8, z: 8, core: 2. Of those that a mesh axis runs over, the one named last changes fastest.
Arguments:
- right_side: float32 [8, 2048, 2048], P('tm', 'space')
- amp_time: float32 [8], P('tm'), may hold values from 0.5 to 2
- amp_space: float32 [2048], replicated
- lin_sky: float32 [2048, 8, 2048], P('space', 'tm'), may hold values from 0.3 to 3
- tile_row: int32 [8, 4096], P('tm', 'space'), may hold values from 0 to 63, as said below
- tile_col: int32 [8, 4096], P('tm', 'space'), may hold values from 0 to 7
- u_frac: float32 [8, 4096, 128], P('tm', 'space'), may hold values from 0 to 128
- v_frac: float32 [8, 4096, 128], P('tm', 'space'), may hold values from 0 to 16
- noise_weight: float32 [8, 4096, 128], P('tm', 'space'), may hold values from 0.005 to 0.05
Outputs:
- solution: float32 [8, 2048, 2048], P('tm', 'space')
- residual: float32 [8, 2048, 2048], P('tm', 'space')
The draws below stay inside these ranges and needn't reach their ends.
Inputs may be any that keep to these rules, and one draw needn't show every extreme that they name: `tile_row`: take the blocks in aligned groups of 1 frames by 64 blocks. Within each group, every range of tile rows from r * 1 to r + 1 - 1 is named by exactly 1 block.
All inputs are finite; a program needn't handle non-finite values.
Results may differ from the reference program's by a relative error of at most 0.00055.
Values sent between devices are 32-bit elements; how exact they have to be, the bound alone decides.
A program may use at most 64 MiB of HBM per device.

```python
import math
import jax
import jax.numpy as jnp
from jax import lax

NX = 2048
FR_DEV = 1
BL_DEV = 64
VB = 128
TV = 16
TU = 128
ITERS = 2
NT = 8
NBL = 4096
NXB = 1024


def draw_right_side(key, part):
    key = jax.random.fold_in(key, 7)
    noise_key, row_key, col_key = jax.random.split(key, 3)
    position = jnp.arange(NX, dtype=jnp.float32)
    rising = jnp.exp(jnp.log(3.0) * position / NX)
    values = jax.random.normal(noise_key, (NT, NX, NX), jnp.float32)
    row_scale = jnp.exp(jax.random.uniform(row_key, (NX,), jnp.float32, 0.0, 0.55))
    col_scale = jnp.exp(jax.random.uniform(col_key, (NX,), jnp.float32, 0.0, 0.55))
    return values * (rising * row_scale)[None, :, None] * col_scale[None, None, :] / 4.0


def draw_amp_space(key, part):
    key = jax.random.fold_in(key, 5)
    frequency = jnp.arange(NX, dtype=jnp.int32)
    folded = jnp.minimum(frequency, NX - frequency).astype(jnp.float32)
    envelope = 1.5 / jnp.sqrt(1.0 + (folded * 32.0 / NX) ** 2)
    rough = jnp.exp(jax.random.uniform(key, (NX,), jnp.float32, -0.69, 0.69))
    return envelope * rough


def draw_tile_row(key, part):
    key = jax.random.fold_in(key, 3)
    first_key, second_key = jax.random.split(key)
    time_groups = NT // FR_DEV
    space_groups = NBL // BL_DEV
    per_group = FR_DEV * BL_DEV // space_groups
    rows_group = NXB // TV // space_groups
    owners_base = jnp.tile(jnp.arange(space_groups, dtype=jnp.int32), per_group)
    device_keys = jax.random.split(first_key, time_groups * space_groups)
    owners = jax.vmap(lambda single: jax.random.permutation(single, owners_base))(device_keys)
    within = jax.random.randint(second_key, owners.shape, 0, rows_group, dtype=jnp.int32)
    chosen = owners * rows_group + within
    chosen = chosen.reshape(time_groups, space_groups, FR_DEV, BL_DEV).transpose(0, 2, 1, 3)
    return chosen.reshape(NT, NBL)


def plant(drawn, rng, low, largest):
    longest = drawn.shape.index(max(drawn.shape))
    spots = []
    for shift in (0, 1):
        where = [jax.random.randint(jax.random.fold_in(rng, axis), (), 0, length) for axis, length in enumerate(drawn.shape)]
        where[longest] = (where[longest] + shift) % drawn.shape[longest]
        spots.append(tuple(where))
    return drawn.at[spots[0]].set(low).at[spots[1]].set(largest)


def block_levels(own_key, dims, cuts, least, largest):
    loudness, own = 1.0, jax.random.fold_in(own_key, 6)
    for dim, blocks in cuts:
        draws = jnp.exp(jax.random.uniform(jax.random.fold_in(own, dim), (blocks,), jnp.float32, least / len(cuts), largest / len(cuts)))
        loudness = loudness * jnp.repeat(draws, dims[dim] // blocks).reshape([-1 if axis == dim else 1 for axis in range(len(dims))])
    return loudness


def setup_inputs(seed: int = 0) -> dict:
    key_of = jax.random.split(jax.random.key(seed), 10)
    return {
        "right_side": draw_right_side(jax.random.fold_in(key_of[9], 71), 0),
        "amp_time": jnp.clip(jnp.exp(math.log(2.0) - 1.3862944 * jax.random.uniform(key_of[1], (NT,), jnp.float32) ** block_levels(key_of[1], (NT,), ((0, 8),), -0.2, 0.2)), 0.5, 2.0),
        "amp_space": draw_amp_space(jax.random.fold_in(key_of[9], 71), 0),
        "lin_sky": jnp.clip(jnp.exp(math.log(3.0) - 2.3025851 * jax.random.uniform(key_of[3], (NX, NT, NX), jnp.float32) ** block_levels(key_of[3], (NX, NT, NX), ((0, 64), (1, 8)), -0.2, 0.2)), 0.3, 3.0),
        "tile_row": draw_tile_row(jax.random.fold_in(key_of[9], 71), 0),
        "tile_col": plant(jax.random.randint(key_of[5], (NT, NBL), 0, NXB // TU), jax.random.fold_in(key_of[5], 1), 0, (NXB // TU) - 1).astype(jnp.int32),
        "u_frac": jnp.clip(128.0 * jax.random.uniform(key_of[6], (NT, NBL, VB), jnp.float32) ** block_levels(key_of[6], (NT, NBL, VB), ((0, 8), (1, 64)), -0.2, 0.2), 0.0, 128.0),
        "v_frac": jnp.clip(16.0 * jax.random.uniform(key_of[7], (NT, NBL, VB), jnp.float32) ** block_levels(key_of[7], (NT, NBL, VB), ((0, 8), (1, 64)), -0.2, 0.2), 0.0, 16.0),
        "noise_weight": jnp.clip(jnp.exp(math.log(0.05) - 2.3025851 * jax.random.uniform(key_of[8], (NT, NBL, VB), jnp.float32) ** block_levels(key_of[8], (NT, NBL, VB), ((0, 8), (1, 64)), -0.2, 0.2)), 0.005, 0.05),
    }


HIGH = lax.Precision.HIGHEST

def hartley_axis(values, dimension):
    length = values.shape[dimension]
    spectrum = jnp.fft.fft(values, axis=dimension)
    return (jnp.real(spectrum) - jnp.imag(spectrum)) / jnp.sqrt(jnp.asarray(length, values.dtype))

def band_rows():
    lower = jnp.arange(NX // 4, dtype=jnp.int32)
    return jnp.concatenate([lower, lower + 3 * NX // 4])

def kernel_tables(u_vals, v_vals):
    cells_v = jnp.arange(TV).astype(u_vals.dtype)
    cells_u = jnp.arange(TU).astype(u_vals.dtype)
    kern_v = jnp.exp(-0.5 * ((cells_v[None, :, None] - v_vals[:, None, :]) / (TV / 4.0)) ** 2)
    kern_u = jnp.exp(-0.5 * ((cells_u[None, None, :] - u_vals[:, :, None]) / (TU / 8.0)) ** 2)
    return (kern_v, kern_u)

def visit_frame(uv_grid, rows_idx, cols_idx, u_vals, v_vals, noise_vals):
    kern_v, kern_u = kernel_tables(u_vals, v_vals)
    tile_view = uv_grid.reshape(NXB // TV, TV, NXB // TU, TU)
    picked = tile_view[rows_idx, :, cols_idx, :]
    product = jnp.einsum('nvu,nmu->nvm', picked, kern_u, precision=HIGH)
    visible = lax.optimization_barrier(jnp.sum(product * kern_v, axis=1))
    weighted = noise_vals * visible
    spread = jnp.einsum('nvm,nmu->nvu', kern_v * weighted[:, None, :], kern_u, precision=HIGH)
    summed = jnp.zeros((NXB // TV, NXB // TU, TV, TU), uv_grid.dtype).at[rows_idx, cols_idx].add(spread)
    return summed.transpose(0, 2, 1, 3).reshape(NXB, NXB)

def reference(right_side, amp_time, amp_space, lin_sky, tile_row, tile_col, u_frac, v_frac, noise_weight):
    band_list = band_rows()
    sky_frames = jnp.transpose(lin_sky, (1, 2, 0))
    outer_scale = amp_space[:, None] * amp_space[None, :]

    def frame_metric(frame_items):
        vector, amp_frame, sky_frame, rows_idx, cols_idx, u_vals, v_vals, noise_vals = frame_items
        prior_scale = amp_frame * outer_scale
        sky_image = hartley_axis(hartley_axis(prior_scale * vector, 1), 0)
        spectrum_full = hartley_axis(hartley_axis(sky_image * sky_frame, 0), 1)
        uv_grid = spectrum_full[band_list][:, band_list]
        spread = visit_frame(uv_grid, rows_idx, cols_idx, u_vals, v_vals, noise_vals)
        padded = jnp.zeros_like(vector).at[band_list[:, None], band_list[None, :]].set(spread)
        image_back = hartley_axis(hartley_axis(padded, 1), 0) * sky_frame
        return vector + prior_scale * hartley_axis(hartley_axis(image_back, 0), 1)

    def metric_apply(vector):
        return lax.map(frame_metric, (vector, amp_time, sky_frames, tile_row, tile_col, u_frac, v_frac, noise_weight))
    solution = jnp.zeros_like(right_side)
    residual = right_side
    direction = right_side
    norm_now = jnp.sum(residual * residual)
    for iteration in range(ITERS):
        applied = metric_apply(direction)
        step_size = norm_now / jnp.sum(direction * applied)
        solution = solution + step_size * direction
        residual = residual - step_size * applied
        if iteration + 1 < ITERS:
            norm_next = jnp.sum(residual * residual)
            direction = residual + norm_next / norm_now * direction
            norm_now = norm_next
    return (solution, residual)
```

```python
import functools
import math

import jax
import jax.numpy as jnp
import ml_dtypes
import numpy as np
from jax import lax
from jax.experimental import pallas as pl
from jax.experimental.pallas import tpu as pltpu
from jax.sharding import PartitionSpec as P

NX = 2048
GROUPS = 64
ROWS = 32
BAND = 16
BLOCKS = 64
CHUNKS = 32
MESH = pl.DeviceIdType.MESH
F32 = jnp.float32
BF16 = jnp.bfloat16

BAND_TILES = list(range(16)) + list(range(48, 64))
BAND_PARTS = [0, 1, 2, 3, 12, 13, 14, 15]

OFFSETS = [(dx, dy, dc) for dx in range(4) for dy in range(8) for dc in range(2)][1:]
OFFSETS.sort(key=lambda o: -(min(o[0], 4 - o[0]) + min(o[1], 8 - o[1])))


class Graph:
    def __init__(self):
        self.terms = []

    def node(self, *terms):
        self.terms.append(terms)
        return len(self.terms) - 1


def real_fourier(graph, inputs):
    n = len(inputs)
    if n == 1:
        return [(inputs[0], None)]
    if n == 2:
        a, b = inputs
        return [(graph.node((1, a), (1, b)), None), (graph.node((1, a), (-1, b)), None)]
    even = real_fourier(graph, inputs[0::2])
    odd = real_fourier(graph, inputs[1::2])
    out = [None] * (n // 2 + 1)
    e, o = even[0][0], odd[0][0]
    out[0] = (graph.node((1, e), (1, o)), None)
    out[n // 2] = (graph.node((1, e), (-1, o)), None)
    for k in range(1, n // 4):
        cos, sin = math.cos(2 * math.pi * k / n), math.sin(2 * math.pi * k / n)
        er, ei = even[k]
        ore, oim = odd[k]
        tr = graph.node((cos, ore), (sin, oim))
        ti = graph.node((cos, oim), (-sin, ore))
        out[k] = (graph.node((1, er), (1, tr)), graph.node((1, ei), (1, ti)))
        out[n // 2 - k] = (graph.node((1, er), (-1, tr)), graph.node((1, ti), (-1, ei)))
    e, o = even[n // 4][0], odd[n // 4][0]
    out[n // 4] = (e, graph.node((-1, o)))
    return out


def fourier_graph(n):
    graph = Graph()
    inputs = [graph.node() for _ in range(n)]
    return graph, inputs, real_fourier(graph, inputs)


def combine(terms):
    terms = [(c, v) for c, v in terms if v is not None]
    if not terms:
        return None
    terms.sort(key=lambda t: t[0] < 0)
    coef, total = terms[0]
    if coef == -1:
        total = -total
    elif coef != 1:
        total = total * coef
    for coef, value in terms[1:]:
        if coef == 1:
            total = total + value
        elif coef == -1:
            total = total - value
        elif coef < 0:
            total = total - value * (-coef)
        else:
            total = total + value * coef
    return total


def forward_fourier(n, values):
    graph, inputs, outputs = fourier_graph(n)
    known = {}
    for index, terms in enumerate(graph.terms):
        if index < n:
            known[index] = values[index]() if values[index] is not None else None
        else:
            known[index] = combine([(c, known[p]) for c, p in terms])
    return [(known[r], known[i] if i is not None else None) for r, i in outputs]


def transposed_fourier(n, pairs, wanted):
    graph, inputs, outputs = fourier_graph(n)
    needed = set(wanted)
    for index, terms in enumerate(graph.terms):
        if any(p in needed for _, p in terms):
            needed.add(index)
    found = {index: [] for index in range(len(graph.terms))}
    for (r, i), (real, imag) in zip(outputs, pairs):
        found[r].append((1, real))
        if i is not None:
            found[i].append((1, imag))
    result = {}
    for index in reversed(range(len(graph.terms))):
        if index not in needed:
            continue
        value = combine(found[index])
        if index < n:
            result[index] = value
        for coef, parent in graph.terms[index]:
            found[parent].append((coef, value))
    return [result[index] for index in wanted]


def halves(table):
    high = table.astype(ml_dtypes.bfloat16)
    low = (table - high.astype(np.float64)).astype(ml_dtypes.bfloat16)
    return np.stack([high, low])


def long_tables():
    b = np.arange(128)
    theta = 2 * np.pi * (b[None, :] * b[:, None] % 128) / 128
    cos, sin = np.cos(theta), np.sin(theta)
    first = np.concatenate([cos + sin, sin - cos], axis=1)
    second = np.concatenate([cos - sin, cos + sin], axis=1)[::-1]
    main = np.concatenate([first, second], axis=0) / math.sqrt(NX)
    angle = 2 * np.pi * (b[None, :] * (8 + 16 * b[:, None]) % NX) / NX
    edge = np.zeros((256, 256))
    edge[:128, :128] = cos + sin
    edge[128:, 128:] = np.cos(angle) + np.sin(angle)
    edge /= math.sqrt(NX)
    phase = 2 * np.pi * np.arange(8)[:, None] * b[None, :] / NX
    twist = np.stack([np.cos(phase), np.sin(phase)]).astype(np.float32)
    return halves(main), halves(edge), twist


def lane_rows():
    lane = np.arange(128)
    return lane // 32, lane % 32


def lane_band():
    lane = np.arange(128)
    return lane // 16 % 4, lane // 64 * 16 + lane % 16


def short_tables(lanes):
    group_in, index_in = lanes
    group_out, index_out = lane_rows()
    same = group_in[:, None] == group_out[None, :]
    theta = 2 * np.pi * (index_in[:, None] * index_out[None, :] % 32) / 32
    mirrored = 2 * np.pi * (index_in[:, None] * (31 - index_out)[None, :] % 32) / 32
    cos, sin = np.cos(theta), np.sin(theta)
    mcos, msin = np.cos(mirrored), np.sin(mirrored)
    top = np.concatenate([same * (cos + sin), same * (mcos - msin)], axis=1)
    bottom = np.concatenate([same * (sin - cos), same * (mcos + msin)], axis=1)
    main = np.concatenate([top, bottom], axis=0) / math.sqrt(NX)
    phase = 2 * np.pi * np.arange(33)[:, None] * index_in[None, :] / NX
    twist = np.stack([np.cos(phase), np.sin(phase)]).astype(np.float32)
    return halves(main), twist


NN = (((1,), (0,)), ((), ()))
NT = (((1,), (1,)), ((), ()))


def split(x):
    high = x.astype(BF16)
    return high, (x - high.astype(F32)).astype(BF16)


def dot(a, b, dims):
    return lax.dot_general(a, b, dims, preferred_element_type=F32)


def product(x, table, dims):
    high, low = split(x)
    return dot(high, table[0], dims) + (dot(high, table[1], dims) + dot(low, table[0], dims))


def product_left(table, x, dims):
    high, low = split(x)
    return dot(table[0], high, dims) + (dot(table[1], high, dims) + dot(table[0], low, dims))


def long_forward(parts, twist, main, edge):
    spectrum = forward_fourier(16, [None if p is None else (lambda p=p: p) for p in parts])
    rows = [jnp.concatenate([spectrum[0][0], spectrum[8][0]], axis=1)]
    for k in range(1, 8):
        real, imag = spectrum[k]
        cos, sin = twist[0, k : k + 1, :], twist[1, k : k + 1, :]
        rows.append(jnp.concatenate([real * cos + imag * sin, imag * cos - real * sin], axis=1))
    size = rows[0].shape[0]
    data = jnp.concatenate(rows, axis=0)
    out = product_left(main, data, NT)
    special = product_left(edge, data[:128], NT)
    lanes = lax.broadcasted_iota(jnp.int32, (256, 128), 1)
    first = jnp.where(lanes < size, special, out[:, :128])
    if size == 16:
        return first
    return jnp.concatenate([first, out[:, 128:]], axis=1)


def long_backward(data, twist, main, edge, wanted):
    turned = data.T
    size = turned.shape[0] // 8
    out = product(turned, main, NN)
    special = product(turned[:size], edge, NN)
    pairs = [(special[:, :128], None)]
    for k in range(1, 8):
        real, imag = out[k * size : (k + 1) * size, :128], out[k * size : (k + 1) * size, 128:]
        cos, sin = twist[0, k : k + 1, :], twist[1, k : k + 1, :]
        pairs.append((real * cos - imag * sin, real * sin + imag * cos))
    pairs.append((special[:, 128:], None))
    return transposed_fourier(16, pairs, wanted)


def short_in(loaders, twist, store):
    spectrum = forward_fourier(64, loaders)
    for k in range(33):
        real, imag = spectrum[k]
        row = (k - 1) % 32 if k < 32 else 32
        if k == 0:
            store(row, real, jnp.zeros_like(real))
            continue
        cos, sin = twist[0, k : k + 1, :], twist[1, k : k + 1, :]
        if k == 32:
            store(row, real * cos, -(real * sin))
        else:
            store(row, real * cos + imag * sin, imag * cos - real * sin)


def short_out(load, twist, wanted):
    pairs = []
    for k in range(33):
        row = (k - 1) % 32 if k < 32 else 32
        real, imag = load(row)
        if k == 0:
            pairs.append((real, None))
            continue
        cos, sin = twist[0, k : k + 1, :], twist[1, k : k + 1, :]
        if k == 32:
            pairs.append((real * cos - imag * sin, None))
        else:
            pairs.append((real * cos - imag * sin, real * sin + imag * cos))
    return transposed_fourier(64, pairs, wanted)


def fold(tile):
    row = lax.broadcasted_iota(jnp.int32, (8, 128), 0)
    lane = lax.broadcasted_iota(jnp.int32, (8, 128), 1)
    other = pltpu.roll(pltpu.roll(tile, 4, 0), 64, 1)
    return jnp.where((row < 4) == (lane < 64), tile, other)


def kernel(
    right_ref, col_ref, row_ref, lin_ref, trow_ref, tcol_ref, u_ref, v_ref, noise_ref,
    long_ref, edge_ref, ltw_ref, short_ref, shortp_ref, stw_ref, stwp_ref,
    sol_ref, res_ref,
    full_out, full_in, half_out, half_in, vis_out, vis_in, lin_in, red_out, red_in,
    kern_u, kern_v, sky, mid, seen, grid_acc, resid,
    full_s, full_r, half_s, half_r, vis_s, vis_r, lin_s, lin_r, red_s, red_r,
):
    me = lax.axis_index("space")
    frame = lax.axis_index("tm")
    mine = (me // 16, me // 2 % 8, me % 2)

    def at(dx, dy, dc):
        return (mine[0] + dx) % 4 * 16 + (mine[1] + dy) % 8 * 2 + (mine[2] + dc) % 2

    def frame_peer(step):
        return (frame + step) % 8

    barrier = pltpu.get_barrier_semaphore()
    for offset in OFFSETS:
        pl.semaphore_signal(barrier, inc=1, device_id=(frame, at(*offset)), device_id_type=MESH)
    for step in range(1, 8):
        pl.semaphore_signal(barrier, inc=1, device_id=(frame_peer(step), me), device_id_type=MESH)

    def send_all(src, dst, send_sem, recv_sem):
        for offset in OFFSETS:
            other = at(*offset)
            pltpu.make_async_remote_copy(
                src_ref=src.at[other], dst_ref=dst.at[me], send_sem=send_sem, recv_sem=recv_sem,
                device_id=(frame, other), device_id_type=MESH,
            ).start()
        pltpu.make_async_copy(src.at[me], dst.at[me], recv_sem).start()

    def arrived(dst, recv_sem):
        pltpu.make_async_copy(dst, dst, recv_sem).wait()

    def sent(src, count, send_sem):
        part = src.at[pl.ds(0, count)]
        pltpu.make_async_copy(part, part, send_sem).wait()

    def reduce_peer(stage, step):
        if stage == 0:
            return (frame, at(step // 2, 0, step % 2))
        if stage == 1:
            return (frame, at(0, step, 0))
        return (frame_peer(step), me)

    def reduce_send(which, stage, value):
        index = which * 3 + stage
        red_out[index] = value
        for step in range(1, 8):
            pltpu.make_async_remote_copy(
                src_ref=red_out.at[index], dst_ref=red_in.at[index, step - 1],
                send_sem=red_s.at[index], recv_sem=red_r.at[index],
                device_id=reduce_peer(stage, step), device_id_type=MESH,
            ).start()

    def reduce_take(which, stage):
        index = which * 3 + stage
        arrived(red_in.at[index], red_r.at[index])
        return red_out[index] + jnp.sum(red_in[index], axis=0)

    def pack(*values):
        lane = lax.broadcasted_iota(jnp.int32, (8, 128), 1)
        row = lax.broadcasted_iota(jnp.int32, (8, 128), 0)
        total = jnp.zeros((8, 128), F32)
        for index, value in enumerate(values):
            total = total + jnp.where((lane == index) & (row == 0), value, 0.0)
        return total

    def unpack(tile, index):
        return tile[0:1, index : index + 1]

    def whole_sum(x):
        return jnp.sum(jnp.sum(x, axis=0, keepdims=True), axis=1, keepdims=True)

    amp_rows = row_ref[...]

    def scaled(ref, a):
        lanes = slice(128 * a, 128 * (a + 1))
        return ref[:, lanes] * (amp_rows * col_ref[:, lanes])

    def rows_to_columns(ref, n):
        out = long_forward([scaled(ref, a) for a in range(16)], ltw_ref, long_ref, edge_ref)
        for g in range(16):
            for h in range(2):
                for l in range(2):
                    full_out[n, 4 * g + 2 * h + l] = out[
                        128 * h + 8 * g : 128 * h + 8 * g + 8, 128 * l : 128 * (l + 1)
                    ]
        send_all(full_out.at[n], full_in.at[n], full_s.at[n], full_r.at[n])

    def store_mid(row, real, imag):
        mid[8 * row : 8 * row + 8, 0:128] = real
        mid[8 * row : 8 * row + 8, 128:256] = imag

    def load_mid(row):
        return mid[8 * row : 8 * row + 8, 0:128], mid[8 * row : 8 * row + 8, 128:256]

    def through_sky(table_in, table_out):
        image = product(mid[...], table_in, NN) * sky[...]
        mid[...] = product(image, table_out, NT)

    def columns_to_band(n):
        arrived(full_in.at[n], full_r.at[n])
        short_in([lambda s=s: full_in[n, s] for s in range(64)], stw_ref, store_mid)
        through_sky(short_ref, shortp_ref)
        tiles = short_out(load_mid, stwp_ref, BAND_TILES)
        for s, tile in enumerate(tiles):
            folded = fold(tile)
            half_out[n, 2 * s] = folded[0:4]
            half_out[n, 2 * s + 1] = folded[4:8]
        send_all(half_out.at[n], half_in.at[n], half_s.at[n], half_r.at[n])

    def pair_of(n, index):
        return fold(jnp.concatenate([half_in[n, 2 * index], half_in[n, 2 * index + 1]], axis=0))

    def band_to_grid(n):
        arrived(half_in.at[n], half_r.at[n])
        rows = [pair_of(n, 2 * g + h) for h in range(2) for g in range(16)]
        parts = long_backward(
            jnp.concatenate(rows, axis=0), ltw_ref, long_ref, edge_ref, BAND_PARTS
        )
        return jnp.concatenate(parts, axis=0)

    def grid_to_band(grid, n):
        parts = [None] * 16
        for index, a in enumerate(BAND_PARTS):
            parts[a] = grid[BAND * index : BAND * (index + 1)]
        out = long_forward(parts, ltw_ref, long_ref, edge_ref)
        for g in range(16):
            for h in range(2):
                folded = fold(out[128 * h + 8 * g : 128 * h + 8 * g + 8])
                half_out[n, 4 * g + 2 * h] = folded[0:4]
                half_out[n, 4 * g + 2 * h + 1] = folded[4:8]
        send_all(half_out.at[n], half_in.at[n], half_s.at[n], half_r.at[n])

    def band_to_columns(n, m):
        arrived(half_in.at[n], half_r.at[n])
        loaders = [None] * 64
        for index, s in enumerate(BAND_TILES):
            loaders[s] = lambda index=index: pair_of(n, index)
        short_in(loaders, stwp_ref, store_mid)
        through_sky(shortp_ref, short_ref)
        tiles = short_out(load_mid, stw_ref, list(range(64)))
        for s, tile in enumerate(tiles):
            full_out[m, s] = tile
        send_all(full_out.at[m], full_in.at[m], full_s.at[m], full_r.at[m])

    def columns_to_rows(n):
        arrived(full_in.at[n], full_r.at[n])
        data = jnp.concatenate(
            [
                jnp.concatenate(
                    [full_in[n, 4 * g + 2 * h + l] for h in range(2) for g in range(16)], axis=0
                )
                for l in range(2)
            ],
            axis=1,
        )
        parts = long_backward(data, ltw_ref, long_ref, edge_ref, list(range(16)))
        return [
            part * (amp_rows * col_ref[:, 128 * a : 128 * (a + 1)]) for a, part in enumerate(parts)
        ]

    def measure(grid, factor, first):
        high, low = split(grid)
        left = jnp.concatenate(
            [
                jnp.concatenate([high, high], axis=1),
                jnp.concatenate([low, jnp.zeros_like(low)], axis=1),
            ],
            axis=0,
        )
        grid_acc[...] = jnp.zeros((256, 256), F32)

        def step(c, total):
            table = kern_u[c]
            both = dot(left, table, NN)
            weights = kern_v[c]
            values = jnp.sum((both[:128] + both[128:]) * weights, axis=0, keepdims=True)
            if first:
                seen[c] = jnp.broadcast_to(values, (8, 256))
            else:
                values = values + factor * seen[c][0:1]
            noise = jnp.concatenate([vis_in[2 * c, 2:3], vis_in[2 * c + 1, 2:3]], axis=1)
            weighed = noise * values
            up, down = split(weights * weighed)
            grid_acc[...] += dot(jnp.concatenate([up, down], axis=0), table, NT)
            return total + weighed * values

        total = lax.fori_loop(0, CHUNKS, step, jnp.zeros((1, 256), F32))
        acc = grid_acc[...]
        return acc[:128, :128] + (acc[:128, 128:] + acc[128:, :128]), whole_sum(total)

    chosen = lax.broadcasted_iota(jnp.int32, (64, 64), 0) == trow_ref[...]
    picker = chosen.astype(BF16)
    columns = jnp.sum(
        jnp.where(chosen, tcol_ref[...].astype(F32), 0.0), axis=1, keepdims=True
    )
    for index, ref in enumerate((u_ref, v_ref, noise_ref)):
        values = ref[...]
        high = values.astype(BF16)
        rest = values - high.astype(F32)
        middle = rest.astype(BF16)
        low = (rest - middle.astype(F32)).astype(BF16)
        vis_out[:, index, :] = (
            dot(picker, high, NN) + dot(picker, middle, NN)
        ) + dot(picker, low, NN)
    vis_out[:, 3, :] = jnp.broadcast_to(columns, (64, 128))

    right_sum = whole_sum(right_ref[...] * right_ref[...])

    pl.semaphore_wait(barrier, len(OFFSETS) + 7)
    rows_to_columns(right_ref, 0)
    send_all(vis_out, vis_in, vis_s, vis_r)
    place = me % 4
    for step in range(1, 4):
        target = (place + step) % 4
        pltpu.make_async_remote_copy(
            src_ref=lin_ref.at[target], dst_ref=lin_in.at[place], send_sem=lin_s, recv_sem=lin_r,
            device_id=(frame, me - place + target), device_id_type=MESH,
        ).start()
    pltpu.make_async_copy(lin_ref.at[place], lin_in.at[place], lin_r).start()

    arrived(vis_in, vis_r)

    def build(c, carry):
        def pair(index):
            return jnp.concatenate(
                [vis_in[2 * c, index : index + 1], vis_in[2 * c + 1, index : index + 1]], axis=1
            )

        cells = lax.broadcasted_iota(jnp.int32, (128, 256), 0).astype(F32)
        away = (cells - pair(0)) * (8.0 / 128)
        high, low = split(jnp.exp(-0.5 * (away * away)))
        kern_u[c, 0:128] = high
        kern_u[c, 128:256] = low
        cells = lax.broadcasted_iota(jnp.int32, (16, 256), 0).astype(F32)
        away = (cells - pair(1)) * (4.0 / 16)
        values = jnp.exp(-0.5 * (away * away))
        column = pair(3)
        for k in range(8):
            kern_v[c, 16 * k : 16 * k + 16] = jnp.where(column == float(k), values, 0.0)
        return carry

    lax.fori_loop(0, CHUNKS, build, 0)

    arrived(lin_in, lin_r)

    def sky_tile(k):
        return jnp.concatenate([lin_in[r, k] for r in range(4)], axis=0)

    for k in range(1, 32):
        sky[8 * (k - 1) : 8 * k, 0:128] = sky_tile(k)
        sky[8 * (k - 1) : 8 * k, 128:256] = sky_tile(64 - k)
    sky[248:256, 0:128] = sky_tile(0)
    sky[256:264, 0:128] = sky_tile(32)
    sky[248:264, 128:256] = jnp.zeros((16, 128), F32)

    columns_to_band(0)
    grid, weight_sum = measure(band_to_grid(0), None, True)
    reduce_send(0, 0, pack(right_sum, weight_sum))
    grid_to_band(grid, 1)
    reduce_send(0, 1, reduce_take(0, 0))
    band_to_columns(1, 1)
    reduce_send(0, 2, reduce_take(0, 1))
    harmonic = columns_to_rows(1)
    sums = reduce_take(0, 2)
    norm_zero = unpack(sums, 0)
    step_zero = norm_zero / (norm_zero + unpack(sums, 1))
    square = jnp.zeros((32, 128), F32)
    cross = jnp.zeros((32, 128), F32)
    for a in range(16):
        lanes = slice(128 * a, 128 * (a + 1))
        before = right_ref[:, lanes]
        after = before - step_zero * (before + harmonic[a])
        resid[:, lanes] = after
        square = square + after * after
        cross = cross + after * before

    reduce_send(1, 0, pack(whole_sum(square), whole_sum(cross)))
    rows_to_columns(resid, 2)
    reduce_send(1, 1, reduce_take(1, 0))
    columns_to_band(2)
    reduce_send(1, 2, reduce_take(1, 1))
    grid = band_to_grid(2)
    sums = reduce_take(1, 2)
    norm_one = unpack(sums, 0)
    growth = norm_one / norm_zero
    squared = norm_one + 2.0 * growth * unpack(sums, 1) + growth * growth * norm_zero
    grid, weight_sum = measure(grid, growth, False)
    reduce_send(2, 0, pack(weight_sum))
    grid_to_band(grid, 3)
    reduce_send(2, 1, reduce_take(2, 0))
    band_to_columns(3, 3)
    reduce_send(2, 2, reduce_take(2, 1))
    harmonic = columns_to_rows(3)
    sums = reduce_take(2, 2)
    step_one = norm_one / (squared + unpack(sums, 0))
    for a in range(16):
        lanes = slice(128 * a, 128 * (a + 1))
        before = right_ref[:, lanes]
        after = resid[:, lanes]
        direction = after + growth * before
        sol_ref[:, lanes] = step_zero * before + step_one * direction
        res_ref[:, lanes] = after - step_one * (direction + harmonic[a])

    for n in range(4):
        sent(full_out.at[n], 63, full_s.at[n])
        sent(half_out.at[n], 63, half_s.at[n])
    sent(vis_out, 63, vis_s)
    sent(lin_ref, 3, lin_s)
    for index in range(9):
        sent(red_in.at[index], 7, red_s.at[index])


def shards(
    right_side, amp_time, amp_space, lin_sky, tile_row, tile_col, u_frac, v_frac, noise_weight
):
    position = lax.axis_index("space")
    amp_rows = lax.dynamic_slice_in_dim(amp_space, position * ROWS, ROWS) * amp_time[0]
    amp_rows = jnp.broadcast_to(amp_rows[:, None], (ROWS, 128))
    order = np.array(list(range(8)) + [8] + [16 - k for k in range(1, 8)])
    sky = lin_sky.reshape(2, 16, 32, 64)[:, order].reshape(2, 2, 2, 4, 32, 64)
    sky = sky.transpose(1, 2, 5, 0, 3, 4).reshape(4, 64, 2, 128)
    long_main, long_edge, long_twist = long_tables()
    short_main, short_twist = short_tables(lane_rows())
    band_main, band_twist = short_tables(lane_band())
    operands = (
        right_side.reshape(ROWS, NX),
        amp_space.reshape(1, NX),
        amp_rows,
        sky,
        tile_row,
        tile_col,
        u_frac.reshape(BLOCKS, 128),
        v_frac.reshape(BLOCKS, 128),
        noise_weight.reshape(BLOCKS, 128),
        *(
            jnp.asarray(t)
            for t in (
                long_main, long_edge, long_twist, short_main, band_main, short_twist, band_twist,
            )
        ),
    )
    vmem = pl.BlockSpec(memory_space=pltpu.VMEM)
    dma = pltpu.SemaphoreType.DMA
    outs = pl.pallas_call(
        kernel,
        out_shape=[jax.ShapeDtypeStruct((ROWS, NX), F32)] * 2,
        in_specs=[vmem] * len(operands),
        out_specs=[vmem] * 2,
        scratch_shapes=[
            pltpu.VMEM((4, 64, 8, 128), F32),
            pltpu.VMEM((4, 64, 8, 128), F32),
            pltpu.VMEM((4, 64, 4, 128), F32),
            pltpu.VMEM((4, 64, 4, 128), F32),
            pltpu.VMEM((64, 4, 128), F32),
            pltpu.VMEM((64, 4, 128), F32),
            pltpu.VMEM((4, 64, 2, 128), F32),
            pltpu.VMEM((9, 8, 128), F32),
            pltpu.VMEM((9, 7, 8, 128), F32),
            pltpu.VMEM((CHUNKS, 256, 256), BF16),
            pltpu.VMEM((CHUNKS, 128, 256), F32),
            pltpu.VMEM((264, 256), F32),
            pltpu.VMEM((264, 256), F32),
            pltpu.VMEM((CHUNKS, 8, 256), F32),
            pltpu.VMEM((256, 256), F32),
            pltpu.VMEM((ROWS, NX), F32),
            dma((4,)), dma((4,)), dma((4,)), dma((4,)),
            dma, dma, dma, dma,
            dma((9,)), dma((9,)),
        ],
        compiler_params=pltpu.CompilerParams(
            collective_id=0, has_side_effects=True, vmem_limit_bytes=48 * 1024 * 1024
        ),
    )(*operands)
    return tuple(out.reshape(1, ROWS, NX) for out in outs)


def solution(mesh):
    in_specs = (
        P("tm", "space", None),
        P("tm"),
        P(),
        P("space", "tm", None),
        P("tm", "space"),
        P("tm", "space"),
        P("tm", "space", None),
        P("tm", "space", None),
        P("tm", "space", None),
    )
    out_specs = (P("tm", "space", None), P("tm", "space", None))
    return jax.shard_map(shards, mesh=mesh, in_specs=in_specs, out_specs=out_specs, check_vma=False)
```

```python
import functools
import math

import jax
import jax.numpy as jnp
import numpy as np
from jax import lax
from jax.experimental import pallas as pl
from jax.experimental.pallas import tpu as pltpu
from jax.sharding import PartitionSpec as P

NX = 2048
GROUPS = 64
ROWS = 32
BAND = 16
BLOCKS = 64
CHUNKS = 32
UNROLL = 16
MESH = pl.DeviceIdType.MESH
F32 = jnp.float32
BF16 = jnp.bfloat16

BAND_TILES = list(range(16)) + list(range(48, 64))
BAND_PARTS = [0, 1, 2, 3, 12, 13, 14, 15]

OFFSETS = [(dx, dy, dc) for dx in range(4) for dy in range(8) for dc in range(2)][1:]
OFFSETS.sort(key=lambda o: -(min(o[0], 4 - o[0]) + min(o[1], 8 - o[1])))


class Graph:
    def __init__(self):
        self.terms = []

    def node(self, *terms):
        self.terms.append(terms)
        return len(self.terms) - 1


def real_fourier(graph, inputs):
    n = len(inputs)
    if n == 1:
        return [(inputs[0], None)]
    if n == 2:
        a, b = inputs
        return [(graph.node((1, a), (1, b)), None), (graph.node((1, a), (-1, b)), None)]
    even = real_fourier(graph, inputs[0::2])
    odd = real_fourier(graph, inputs[1::2])
    out = [None] * (n // 2 + 1)
    e, o = even[0][0], odd[0][0]
    out[0] = (graph.node((1, e), (1, o)), None)
    out[n // 2] = (graph.node((1, e), (-1, o)), None)
    for k in range(1, n // 4):
        cos, sin = math.cos(2 * math.pi * k / n), math.sin(2 * math.pi * k / n)
        er, ei = even[k]
        ore, oim = odd[k]
        tr = graph.node((cos, ore), (sin, oim))
        ti = graph.node((cos, oim), (-sin, ore))
        out[k] = (graph.node((1, er), (1, tr)), graph.node((1, ei), (1, ti)))
        out[n // 2 - k] = (graph.node((1, er), (-1, tr)), graph.node((1, ti), (-1, ei)))
    e, o = even[n // 4][0], odd[n // 4][0]
    out[n // 4] = (e, graph.node((-1, o)))
    return out


def fourier_graph(n):
    graph = Graph()
    inputs = [graph.node() for _ in range(n)]
    return graph, inputs, real_fourier(graph, inputs)


def combine(terms):
    terms = [(c, v) for c, v in terms if v is not None]
    if not terms:
        return None
    terms.sort(key=lambda t: t[0] < 0)
    coef, total = terms[0]
    if coef == -1:
        total = -total
    elif coef != 1:
        total = total * coef
    for coef, value in terms[1:]:
        if coef == 1:
            total = total + value
        elif coef == -1:
            total = total - value
        elif coef < 0:
            total = total - value * (-coef)
        else:
            total = total + value * coef
    return total


def forward_fourier(n, values):
    graph, inputs, outputs = fourier_graph(n)
    known = {}
    for index, terms in enumerate(graph.terms):
        if index < n:
            known[index] = values[index]() if values[index] is not None else None
        else:
            known[index] = combine([(c, known[p]) for c, p in terms])
    return [(known[r], known[i] if i is not None else None) for r, i in outputs]


def transposed_fourier(n, pairs, wanted):
    graph, inputs, outputs = fourier_graph(n)
    needed = set(wanted)
    for index, terms in enumerate(graph.terms):
        if any(p in needed for _, p in terms):
            needed.add(index)
    found = {index: [] for index in range(len(graph.terms))}
    for (r, i), (real, imag) in zip(outputs, pairs):
        found[r].append((1, real))
        if i is not None:
            found[i].append((1, imag))
    result = {}
    for index in reversed(range(len(graph.terms))):
        if index not in needed:
            continue
        value = combine(found[index])
        if index < n:
            result[index] = value
        for coef, parent in graph.terms[index]:
            found[parent].append((coef, value))
    return [result[index] for index in wanted]


def long_tables():
    b = np.arange(128)
    theta = 2 * np.pi * (b[None, :] * b[:, None] % 128) / 128
    cos, sin = np.cos(theta), np.sin(theta)
    first = np.concatenate([cos + sin, sin - cos], axis=1)
    second = np.concatenate([cos - sin, cos + sin], axis=1)[::-1]
    main = np.concatenate([first, second], axis=0) / math.sqrt(NX)
    angle = 2 * np.pi * (b[None, :] * (8 + 16 * b[:, None]) % NX) / NX
    edge = np.zeros((256, 256))
    edge[:128, :128] = cos + sin
    edge[128:, 128:] = np.cos(angle) + np.sin(angle)
    edge /= math.sqrt(NX)
    phase = 2 * np.pi * np.arange(8)[:, None] * b[None, :] / NX
    twist = np.stack([np.cos(phase), np.sin(phase)]).astype(np.float32)
    return main.astype(np.float32), edge.astype(np.float32), twist


def lane_rows():
    lane = np.arange(128)
    return lane // 32, lane % 32


def lane_band():
    lane = np.arange(128)
    return lane // 16 % 4, lane // 64 * 16 + lane % 16


def short_tables(lanes):
    group_in, index_in = lanes
    group_out, index_out = lane_rows()
    same = group_in[:, None] == group_out[None, :]
    theta = 2 * np.pi * (index_in[:, None] * index_out[None, :] % 32) / 32
    mirrored = 2 * np.pi * (index_in[:, None] * (31 - index_out)[None, :] % 32) / 32
    cos, sin = np.cos(theta), np.sin(theta)
    mcos, msin = np.cos(mirrored), np.sin(mirrored)
    top = np.concatenate([same * (cos + sin), same * (mcos - msin)], axis=1)
    bottom = np.concatenate([same * (sin - cos), same * (mcos + msin)], axis=1)
    main = np.concatenate([top, bottom], axis=0) / math.sqrt(NX)
    phase = 2 * np.pi * np.arange(33)[:, None] * index_in[None, :] / NX
    twist = np.stack([np.cos(phase), np.sin(phase)]).astype(np.float32)
    return main.astype(np.float32), twist


NN = (((1,), (0,)), ((), ()))
NT = (((1,), (1,)), ((), ()))


def split(x):
    high = x.astype(BF16)
    return high, (x - high.astype(F32)).astype(BF16)


def dot(a, b, dims):
    return lax.dot_general(a, b, dims, preferred_element_type=F32)


def product(x, table, dims):
    high, low = split(x)
    return dot(high, table[0], dims) + (dot(high, table[1], dims) + dot(low, table[0], dims))


def product_left(table, x, dims):
    high, low = split(x)
    return dot(table[0], high, dims) + (dot(table[1], high, dims) + dot(table[0], low, dims))


def long_forward(parts, twist, main, edge):
    spectrum = forward_fourier(16, [None if p is None else (lambda p=p: p) for p in parts])
    rows = [jnp.concatenate([spectrum[0][0], spectrum[8][0]], axis=1)]
    for k in range(1, 8):
        real, imag = spectrum[k]
        cos, sin = twist[0, k : k + 1, :], twist[1, k : k + 1, :]
        rows.append(jnp.concatenate([real * cos + imag * sin, imag * cos - real * sin], axis=1))
    size = rows[0].shape[0]
    data = jnp.concatenate(rows, axis=0)
    out = product_left(main, data, NT)
    special = product_left(edge, data[:128], NT)
    lanes = lax.broadcasted_iota(jnp.int32, (256, 128), 1)
    first = jnp.where(lanes < size, special, out[:, :128])
    if size == 16:
        return first
    return jnp.concatenate([first, out[:, 128:]], axis=1)


def long_backward(data, twist, main, edge, wanted):
    turned = data.T
    size = turned.shape[0] // 8
    out = product(turned, main, NN)
    special = product(turned[:size], edge, NN)
    pairs = [(special[:, :128], None)]
    for k in range(1, 8):
        real, imag = out[k * size : (k + 1) * size, :128], out[k * size : (k + 1) * size, 128:]
        cos, sin = twist[0, k : k + 1, :], twist[1, k : k + 1, :]
        pairs.append((real * cos - imag * sin, real * sin + imag * cos))
    pairs.append((special[:, 128:], None))
    return transposed_fourier(16, pairs, wanted)


def short_in(loaders, twist, store):
    spectrum = forward_fourier(64, loaders)
    for k in range(33):
        real, imag = spectrum[k]
        row = (k - 1) % 32 if k < 32 else 32
        if k == 0:
            store(row, real, jnp.zeros_like(real))
            continue
        cos, sin = twist[0, k : k + 1, :], twist[1, k : k + 1, :]
        if k == 32:
            store(row, real * cos, -(real * sin))
        else:
            store(row, real * cos + imag * sin, imag * cos - real * sin)


def short_out(load, twist, wanted):
    pairs = []
    for k in range(33):
        row = (k - 1) % 32 if k < 32 else 32
        real, imag = load(row)
        if k == 0:
            pairs.append((real, None))
            continue
        cos, sin = twist[0, k : k + 1, :], twist[1, k : k + 1, :]
        if k == 32:
            pairs.append((real * cos - imag * sin, None))
        else:
            pairs.append((real * cos - imag * sin, real * sin + imag * cos))
    return transposed_fourier(64, pairs, wanted)


def fold(tile):
    row = lax.broadcasted_iota(jnp.int32, (8, 128), 0)
    lane = lax.broadcasted_iota(jnp.int32, (8, 128), 1)
    other = pltpu.roll(pltpu.roll(tile, 4, 0), 64, 1)
    return jnp.where((row < 4) == (lane < 64), tile, other)


def kernel(
    right_hbm, time_hbm, col_hbm, lin_hbm, trow_hbm, tcol_hbm, u_hbm, v_hbm, noise_hbm, order_hbm,
    long_hbm, edge_hbm, ltw_hbm, short_hbm, shortp_hbm, stw_hbm, stwp_hbm,
    sol_ref, res_ref,
    right_ref, time_ref, col_ref, raw_ref, trow_ref, tcol_ref, u_ref, v_ref, noise_ref, order_ref,
    long_ref, edge_ref, ltw_ref, short_ref, shortp_ref, stw_ref, stwp_ref,
    long_tab, edge_tab, short_tab, shortp_tab, row_ref, turned, lin_ref,
    full_out, full_in, half_out, half_in, vis_out, vis_in, lin_in, red_out, red_in,
    kern_u, kern_v, sky, mid, seen, resid,
    full_s, full_r, half_s, half_r, vis_s, vis_r, lin_s, lin_r, red_s, red_r, load_s,
):
    me = lax.axis_index("space")
    frame = lax.axis_index("tm")
    mine = (me // 16, me // 2 % 8, me % 2)

    def at(dx, dy, dc):
        return (mine[0] + dx) % 4 * 16 + (mine[1] + dy) % 8 * 2 + (mine[2] + dc) % 2

    def frame_peer(step):
        return (frame + step) % 8

    barrier = pltpu.get_barrier_semaphore()
    for offset in OFFSETS:
        pl.semaphore_signal(barrier, inc=1, device_id=(frame, at(*offset)), device_id_type=MESH)
    for step in range(1, 8):
        pl.semaphore_signal(barrier, inc=1, device_id=(frame_peer(step), me), device_id_type=MESH)

    loads = [
        pltpu.make_async_copy(src, dst, load_s.at[index])
        for index, (src, dst) in enumerate(
            (
                (right_hbm.at[0], right_ref),
                (time_hbm, time_ref),
                (col_hbm, col_ref),
                (ltw_hbm, ltw_ref),
                (long_hbm, long_ref),
                (edge_hbm, edge_ref),
                (lin_hbm.at[:, 0, :], raw_ref),
                (order_hbm, order_ref),
                (trow_hbm, trow_ref),
                (tcol_hbm, tcol_ref),
                (u_hbm.at[0], u_ref),
                (v_hbm.at[0], v_ref),
                (noise_hbm.at[0], noise_ref),
                (short_hbm, short_ref),
                (shortp_hbm, shortp_ref),
                (stw_hbm, stw_ref),
                (stwp_hbm, stwp_ref),
            )
        )
    ]
    for load in loads:
        load.start()

    def send_all(src, dst, send_sem, recv_sem):
        for offset in OFFSETS:
            other = at(*offset)
            pltpu.make_async_remote_copy(
                src_ref=src.at[other], dst_ref=dst.at[me], send_sem=send_sem, recv_sem=recv_sem,
                device_id=(frame, other), device_id_type=MESH,
            ).start()
        pltpu.make_async_copy(src.at[me], dst.at[me], recv_sem).start()

    def arrived(dst, recv_sem):
        pltpu.make_async_copy(dst, dst, recv_sem).wait()

    def sent(src, count, send_sem):
        part = src.at[pl.ds(0, count)]
        pltpu.make_async_copy(part, part, send_sem).wait()

    def reduce_peer(stage, step):
        if stage == 0:
            return (frame, at(step // 2, 0, step % 2))
        if stage == 1:
            return (frame, at(0, step, 0))
        return (frame_peer(step), me)

    def reduce_send(which, stage, value):
        index = which * 3 + stage
        red_out[index] = value
        for step in range(1, 8):
            pltpu.make_async_remote_copy(
                src_ref=red_out.at[index], dst_ref=red_in.at[index, step - 1],
                send_sem=red_s.at[index], recv_sem=red_r.at[index],
                device_id=reduce_peer(stage, step), device_id_type=MESH,
            ).start()

    def reduce_take(which, stage):
        index = which * 3 + stage
        arrived(red_in.at[index], red_r.at[index])
        return red_out[index] + jnp.sum(red_in[index], axis=0)

    def pack(*values):
        lane = lax.broadcasted_iota(jnp.int32, (8, 128), 1)
        row = lax.broadcasted_iota(jnp.int32, (8, 128), 0)
        total = jnp.zeros((8, 128), F32)
        for index, value in enumerate(values):
            total = total + jnp.where((lane == index) & (row == 0), value, 0.0)
        return total

    def unpack(tile, index):
        return tile[0:1, index : index + 1]

    def whole_sum(x):
        return jnp.sum(jnp.sum(x, axis=0, keepdims=True), axis=1, keepdims=True)

    def scale(a):
        return row_ref[...] * col_ref[:, 128 * a : 128 * (a + 1)]

    def scaled(ref, a):
        return ref[:, 128 * a : 128 * (a + 1)] * scale(a)

    def rows_to_columns(ref, n):
        out = long_forward([scaled(ref, a) for a in range(16)], ltw_ref, long_tab, edge_tab)
        for g in range(16):
            for h in range(2):
                for l in range(2):
                    full_out[n, 4 * g + 2 * h + l] = out[
                        128 * h + 8 * g : 128 * h + 8 * g + 8, 128 * l : 128 * (l + 1)
                    ]

    def send_full(n):
        send_all(full_out.at[n], full_in.at[n], full_s.at[n], full_r.at[n])

    def store_mid(row, real, imag):
        mid[8 * row : 8 * row + 8, 0:128] = real
        mid[8 * row : 8 * row + 8, 128:256] = imag

    def load_mid(row):
        return mid[8 * row : 8 * row + 8, 0:128], mid[8 * row : 8 * row + 8, 128:256]

    def through_sky(table_in, table_out):
        image = product(mid[...], table_in, NN) * sky[...]
        mid[...] = product(image, table_out, NT)

    def columns_to_band(n):
        arrived(full_in.at[n], full_r.at[n])
        short_in([lambda s=s: full_in[n, s] for s in range(64)], stw_ref, store_mid)
        through_sky(short_tab, shortp_tab)
        tiles = short_out(load_mid, stwp_ref, BAND_TILES)
        for s, tile in enumerate(tiles):
            folded = fold(tile)
            half_out[n, 2 * s] = folded[0:4]
            half_out[n, 2 * s + 1] = folded[4:8]
        send_all(half_out.at[n], half_in.at[n], half_s.at[n], half_r.at[n])

    def pair_of(n, index):
        return fold(jnp.concatenate([half_in[n, 2 * index], half_in[n, 2 * index + 1]], axis=0))

    def band_to_grid(n):
        arrived(half_in.at[n], half_r.at[n])
        rows = [pair_of(n, 2 * g + h) for h in range(2) for g in range(16)]
        parts = long_backward(
            jnp.concatenate(rows, axis=0), ltw_ref, long_tab, edge_tab, BAND_PARTS
        )
        return jnp.concatenate(parts, axis=0)

    def grid_to_band(grid, n):
        parts = [None] * 16
        for index, a in enumerate(BAND_PARTS):
            parts[a] = grid[BAND * index : BAND * (index + 1)]
        out = long_forward(parts, ltw_ref, long_tab, edge_tab)
        for g in range(16):
            for h in range(2):
                folded = fold(out[128 * h + 8 * g : 128 * h + 8 * g + 8])
                half_out[n, 4 * g + 2 * h] = folded[0:4]
                half_out[n, 4 * g + 2 * h + 1] = folded[4:8]
        send_all(half_out.at[n], half_in.at[n], half_s.at[n], half_r.at[n])

    def band_to_columns(n, m):
        arrived(half_in.at[n], half_r.at[n])
        loaders = [None] * 64
        for index, s in enumerate(BAND_TILES):
            loaders[s] = lambda index=index: pair_of(n, index)
        short_in(loaders, stwp_ref, store_mid)
        through_sky(shortp_tab, short_tab)
        tiles = short_out(load_mid, stw_ref, list(range(64)))
        for s, tile in enumerate(tiles):
            full_out[m, s] = tile
        send_full(m)

    def columns_to_rows(n):
        arrived(full_in.at[n], full_r.at[n])
        data = jnp.concatenate(
            [
                jnp.concatenate(
                    [full_in[n, 4 * g + 2 * h + l] for h in range(2) for g in range(16)], axis=0
                )
                for l in range(2)
            ],
            axis=1,
        )
        parts = long_backward(data, ltw_ref, long_tab, edge_tab, list(range(16)))
        return [part * scale(a) for a, part in enumerate(parts)]

    def measure(grid, factor, first):
        tiles = [grid[BAND * k : BAND * (k + 1)] for k in range(8)]
        zero = jnp.zeros((BAND, 128), BF16)

        def step(start, carry):
            total, sums = carry[0], list(carry[1:])
            for c in [start * UNROLL + index for index in range(UNROLL)]:
                table = kern_u[c]
                weights = kern_v[c]
                columns, rows = [], []
                for block in (2 * c, 2 * c + 1):
                    column = vis_in[block, 3:4]
                    tile = tiles[0]
                    for k in range(1, 8):
                        tile = jnp.where(column == float(k), tiles[k], tile)
                    high, low = split(tile)
                    columns.append(column)
                    rows.append(jnp.concatenate([high, high], axis=1))
                    rows.append(jnp.concatenate([low, zero], axis=1))
                both = dot(jnp.concatenate(rows, axis=0), table, NN)
                picked = jnp.concatenate(
                    [both[0:16, :128] + both[16:32, :128], both[32:48, 128:] + both[48:64, 128:]],
                    axis=1,
                )
                values = jnp.sum(picked * weights, axis=0, keepdims=True)
                if first:
                    seen[c] = jnp.broadcast_to(values, (8, 256))
                else:
                    values = values + factor * seen[c][0:1]
                noise = jnp.concatenate([vis_in[2 * c, 2:3], vis_in[2 * c + 1, 2:3]], axis=1)
                weighed = noise * values
                total = total + weighed * values
                up, down = split(weights * weighed)
                spread = jnp.concatenate(
                    [
                        jnp.concatenate([up[:, :128], zero], axis=1),
                        jnp.concatenate([down[:, :128], zero], axis=1),
                        jnp.concatenate([zero, up[:, 128:]], axis=1),
                        jnp.concatenate([zero, down[:, 128:]], axis=1),
                    ],
                    axis=0,
                )
                back = dot(spread, table, NT)
                for index, column in enumerate(columns):
                    high = back[32 * index : 32 * index + 16]
                    low = back[32 * index + 16 : 32 * index + 32]
                    tile = high[:, :128] + (high[:, 128:] + low[:, :128])
                    for k in range(8):
                        sums[k] = sums[k] + jnp.where(column == float(k), tile, 0.0)
            return (total, *sums)

        empty = [jnp.zeros((1, 256), F32)] + [jnp.zeros((BAND, 128), F32)] * 8
        total, *sums = lax.fori_loop(0, CHUNKS // UNROLL, step, tuple(empty))
        return jnp.concatenate(sums, axis=0), whole_sum(total)

    def exact(picker, values):
        high = values.astype(BF16)
        rest = values - high.astype(F32)
        middle = rest.astype(BF16)
        low = (rest - middle.astype(F32)).astype(BF16)
        return (dot(picker, high, NN) + dot(picker, middle, NN)) + dot(picker, low, NN)

    def both_parts(table, parts):
        parts[0], parts[1] = split(table[...])

    for load in loads[:6]:
        load.wait()
    columns = lax.broadcasted_iota(jnp.int32, (ROWS, NX), 1)
    rows = lax.broadcasted_iota(jnp.int32, (ROWS, NX), 0)
    amp_rows = jnp.sum(
        jnp.where(columns == me * ROWS + rows, col_ref[...], 0.0), axis=1, keepdims=True
    )
    row_ref[...] = jnp.broadcast_to(amp_rows * time_ref[...], (ROWS, 128))
    both_parts(long_ref, long_tab)
    both_parts(edge_ref, edge_tab)
    rows_to_columns(right_ref, 0)
    right_sum = whole_sum(right_ref[...] * right_ref[...])

    for load in loads[8:13]:
        load.wait()
    chosen = lax.broadcasted_iota(jnp.int32, (64, 64), 0) == trow_ref[...]
    picker = chosen.astype(BF16)
    columns = jnp.sum(
        jnp.where(chosen, tcol_ref[...].astype(F32), 0.0), axis=1, keepdims=True
    )
    for index, ref in enumerate((u_ref, v_ref, noise_ref)):
        vis_out[:, index, :] = exact(picker, ref[...])
    vis_out[:, 3, :] = jnp.broadcast_to(columns, (64, 128))

    for load in loads[6:8]:
        load.wait()
    ordered = exact(order_ref[...].astype(BF16), raw_ref[...])
    for c in range(16):
        turned[128 * c : 128 * (c + 1), 0:32] = ordered[:, 128 * c : 128 * (c + 1)].T
    for a in range(16):
        four = jnp.concatenate(
            [turned[pl.ds(4 * a + r, 32, stride=64), 0:32] for r in range(4)], axis=1
        )
        back = four.T
        for r in range(4):
            tile = jnp.concatenate(
                [back[32 * r + 8 * k : 32 * r + 8 * k + 8] for k in range(4)], axis=1
            )
            for hl in range(4):
                lin_ref[hl, 4 * a + r] = tile[2 * hl : 2 * hl + 2]

    for load in loads[13:]:
        load.wait()
    both_parts(short_ref, short_tab)
    both_parts(shortp_ref, shortp_tab)
    pl.semaphore_wait(barrier, len(OFFSETS) + 7)
    send_full(0)
    place = me % 4
    for step in range(1, 4):
        target = (place + step) % 4
        pltpu.make_async_remote_copy(
            src_ref=lin_ref.at[target], dst_ref=lin_in.at[place], send_sem=lin_s, recv_sem=lin_r,
            device_id=(frame, me - place + target), device_id_type=MESH,
        ).start()
    pltpu.make_async_copy(lin_ref.at[place], lin_in.at[place], lin_r).start()
    send_all(vis_out, vis_in, vis_s, vis_r)

    def build(c, carry):
        def pair(index):
            return jnp.concatenate(
                [vis_in[2 * c, index : index + 1], vis_in[2 * c + 1, index : index + 1]], axis=1
            )

        cells = lax.broadcasted_iota(jnp.int32, (128, 256), 0).astype(F32)
        away = (cells - pair(0)) * (8.0 / 128)
        high, low = split(jnp.exp(-0.5 * (away * away)))
        kern_u[c, 0:128] = high
        kern_u[c, 128:256] = low
        cells = lax.broadcasted_iota(jnp.int32, (16, 256), 0).astype(F32)
        away = (cells - pair(1)) * (4.0 / 16)
        kern_v[c] = jnp.exp(-0.5 * (away * away))
        return carry

    arrived(lin_in, lin_r)

    def sky_tile(k):
        return jnp.concatenate([lin_in[r, k] for r in range(4)], axis=0)

    for k in range(1, 32):
        sky[8 * (k - 1) : 8 * k, 0:128] = sky_tile(k)
        sky[8 * (k - 1) : 8 * k, 128:256] = sky_tile(64 - k)
    sky[248:256, 0:128] = sky_tile(0)
    sky[256:264, 0:128] = sky_tile(32)
    sky[248:264, 128:256] = jnp.zeros((16, 128), F32)

    columns_to_band(0)
    arrived(vis_in, vis_r)
    lax.fori_loop(0, CHUNKS, build, 0)
    grid, weight_sum = measure(band_to_grid(0), None, True)
    reduce_send(0, 0, pack(right_sum, weight_sum))
    grid_to_band(grid, 1)
    reduce_send(0, 1, reduce_take(0, 0))
    band_to_columns(1, 1)
    reduce_send(0, 2, reduce_take(0, 1))
    harmonic = columns_to_rows(1)
    sums = reduce_take(0, 2)
    norm_zero = unpack(sums, 0)
    step_zero = norm_zero / (norm_zero + unpack(sums, 1))
    square = jnp.zeros((32, 128), F32)
    cross = jnp.zeros((32, 128), F32)
    for a in range(16):
        lanes = slice(128 * a, 128 * (a + 1))
        before = right_ref[:, lanes]
        after = before - step_zero * (before + harmonic[a])
        resid[:, lanes] = after
        square = square + after * after
        cross = cross + after * before

    reduce_send(1, 0, pack(whole_sum(square), whole_sum(cross)))
    rows_to_columns(resid, 2)
    send_full(2)
    reduce_send(1, 1, reduce_take(1, 0))
    columns_to_band(2)
    reduce_send(1, 2, reduce_take(1, 1))
    grid = band_to_grid(2)
    sums = reduce_take(1, 2)
    norm_one = unpack(sums, 0)
    growth = norm_one / norm_zero
    squared = norm_one + 2.0 * growth * unpack(sums, 1) + growth * growth * norm_zero
    grid, weight_sum = measure(grid, growth, False)
    reduce_send(2, 0, pack(weight_sum))
    grid_to_band(grid, 3)
    reduce_send(2, 1, reduce_take(2, 0))
    band_to_columns(3, 3)
    reduce_send(2, 2, reduce_take(2, 1))
    harmonic = columns_to_rows(3)
    sums = reduce_take(2, 2)
    step_one = norm_one / (squared + unpack(sums, 0))
    for a in range(16):
        lanes = slice(128 * a, 128 * (a + 1))
        before = right_ref[:, lanes]
        after = resid[:, lanes]
        direction = after + growth * before
        sol_ref[:, lanes] = step_zero * before + step_one * direction
        res_ref[:, lanes] = after - step_one * (direction + harmonic[a])

    for n in range(4):
        sent(full_out.at[n], 63, full_s.at[n])
        sent(half_out.at[n], 63, half_s.at[n])
    sent(vis_out, 63, vis_s)
    sent(lin_ref, 3, lin_s)
    for index in range(9):
        sent(red_in.at[index], 7, red_s.at[index])


def shards(
    right_side, amp_time, amp_space, lin_sky, tile_row, tile_col, u_frac, v_frac, noise_weight
):
    order = np.zeros((32, 32))
    for row, (kappa, half, left, k2) in enumerate(np.ndindex(4, 2, 2, 2)):
        index = 4 * left + kappa
        k1 = index if half == 0 else 8 if index == 0 else 16 - index
        order[row, 16 * k2 + k1] = 1.0
    long_main, long_edge, long_twist = long_tables()
    short_main, short_twist = short_tables(lane_rows())
    band_main, band_twist = short_tables(lane_band())
    operands = (
        right_side,
        amp_time.reshape(1, 1),
        amp_space.reshape(1, NX),
        lin_sky,
        tile_row,
        tile_col,
        u_frac,
        v_frac,
        noise_weight,
        jnp.asarray(order, F32),
        *(
            jnp.asarray(t)
            for t in (
                long_main, long_edge, long_twist, short_main, band_main, short_twist, band_twist,
            )
        ),
    )
    vmem = pl.BlockSpec(memory_space=pltpu.VMEM)
    dma = pltpu.SemaphoreType.DMA
    outs = pl.pallas_call(
        kernel,
        out_shape=[jax.ShapeDtypeStruct((ROWS, NX), F32)] * 2,
        in_specs=[pl.BlockSpec(memory_space=pltpu.MemorySpace.HBM)] * len(operands),
        out_specs=[vmem] * 2,
        scratch_shapes=[
            pltpu.VMEM((ROWS, NX), F32),
            *(pltpu.VMEM(o.shape, o.dtype) for o in operands[1:3]),
            pltpu.VMEM((ROWS, NX), F32),
            *(pltpu.VMEM(o.shape, o.dtype) for o in operands[4:6]),
            *[pltpu.VMEM((BLOCKS, 128), F32)] * 3,
            *(pltpu.VMEM(o.shape, o.dtype) for o in operands[9:]),
            *[pltpu.VMEM((2, 256, 256), BF16)] * 4,
            pltpu.VMEM((ROWS, 128), F32),
            pltpu.VMEM((NX, 128), F32),
            pltpu.VMEM((4, 64, 2, 128), F32),
            pltpu.VMEM((4, 64, 8, 128), F32),
            pltpu.VMEM((4, 64, 8, 128), F32),
            pltpu.VMEM((4, 64, 4, 128), F32),
            pltpu.VMEM((4, 64, 4, 128), F32),
            pltpu.VMEM((64, 4, 128), F32),
            pltpu.VMEM((64, 4, 128), F32),
            pltpu.VMEM((4, 64, 2, 128), F32),
            pltpu.VMEM((9, 8, 128), F32),
            pltpu.VMEM((9, 7, 8, 128), F32),
            pltpu.VMEM((CHUNKS, 256, 256), BF16),
            pltpu.VMEM((CHUNKS, BAND, 256), F32),
            pltpu.VMEM((264, 256), F32),
            pltpu.VMEM((264, 256), F32),
            pltpu.VMEM((CHUNKS, 8, 256), F32),
            pltpu.VMEM((ROWS, NX), F32),
            dma((4,)), dma((4,)), dma((4,)), dma((4,)),
            dma, dma, dma, dma,
            dma((9,)), dma((9,)), dma((17,)),
        ],
        compiler_params=pltpu.CompilerParams(
            collective_id=0, has_side_effects=True, vmem_limit_bytes=63 * 1024 * 1024
        ),
    )(*operands)
    return tuple(out.reshape(1, ROWS, NX) for out in outs)


def solution(mesh):
    in_specs = (
        P("tm", "space", None),
        P("tm"),
        P(),
        P("space", "tm", None),
        P("tm", "space"),
        P("tm", "space"),
        P("tm", "space", None),
        P("tm", "space", None),
        P("tm", "space", None),
    )
    out_specs = (P("tm", "space", None), P("tm", "space", None))
    return jax.shard_map(shards, mesh=mesh, in_specs=in_specs, out_specs=out_specs, check_vma=False)
```

```python
import functools
import math

import jax
import jax.numpy as jnp
import numpy as np
from jax import lax
from jax.experimental import pallas as pl
from jax.experimental.pallas import tpu as pltpu
from jax.sharding import PartitionSpec as P

NX = 2048
GROUPS = 64
ROWS = 32
BAND = 16
BLOCKS = 64
CHUNKS = 32
UNROLL = 16
MESH = pl.DeviceIdType.MESH
F32 = jnp.float32
BF16 = jnp.bfloat16

BAND_TILES = list(range(16)) + list(range(48, 64))
BAND_PARTS = [0, 1, 2, 3, 12, 13, 14, 15]

ORDER = [
    40, 41, 42, 25, 57, 38, 39, 43, 24, 56, 59, 37, 44, 27, 9, 36,
    23, 22, 8, 45, 26, 54, 58, 55, 10, 7, 21, 34, 47, 46, 29, 35,
    28, 60, 53, 20, 52, 11, 6, 61, 50, 32, 31, 30, 5, 19, 13, 51,
    12, 18, 63, 33, 4, 62, 16, 49, 15, 2, 3, 14, 17, 48, 1,
]
OFFSETS = [(code // 16, code // 2 % 8, code % 2) for code in ORDER]


class Graph:
    def __init__(self):
        self.terms = []

    def node(self, *terms):
        self.terms.append(terms)
        return len(self.terms) - 1


def real_fourier(graph, inputs):
    n = len(inputs)
    if n == 1:
        return [(inputs[0], None)]
    if n == 2:
        a, b = inputs
        return [(graph.node((1, a), (1, b)), None), (graph.node((1, a), (-1, b)), None)]
    even = real_fourier(graph, inputs[0::2])
    odd = real_fourier(graph, inputs[1::2])
    out = [None] * (n // 2 + 1)
    e, o = even[0][0], odd[0][0]
    out[0] = (graph.node((1, e), (1, o)), None)
    out[n // 2] = (graph.node((1, e), (-1, o)), None)
    for k in range(1, n // 4):
        cos, sin = math.cos(2 * math.pi * k / n), math.sin(2 * math.pi * k / n)
        er, ei = even[k]
        ore, oim = odd[k]
        tr = graph.node((cos, ore), (sin, oim))
        ti = graph.node((cos, oim), (-sin, ore))
        out[k] = (graph.node((1, er), (1, tr)), graph.node((1, ei), (1, ti)))
        out[n // 2 - k] = (graph.node((1, er), (-1, tr)), graph.node((1, ti), (-1, ei)))
    e, o = even[n // 4][0], odd[n // 4][0]
    out[n // 4] = (e, graph.node((-1, o)))
    return out


def fourier_graph(n):
    graph = Graph()
    inputs = [graph.node() for _ in range(n)]
    return graph, inputs, real_fourier(graph, inputs)


def combine(terms):
    terms = [(c, v) for c, v in terms if v is not None]
    if not terms:
        return None
    terms.sort(key=lambda t: t[0] < 0)
    coef, total = terms[0]
    if coef == -1:
        total = -total
    elif coef != 1:
        total = total * coef
    for coef, value in terms[1:]:
        if coef == 1:
            total = total + value
        elif coef == -1:
            total = total - value
        elif coef < 0:
            total = total - value * (-coef)
        else:
            total = total + value * coef
    return total


def forward_fourier(n, values):
    graph, inputs, outputs = fourier_graph(n)
    known = {}
    for index, terms in enumerate(graph.terms):
        if index < n:
            known[index] = values[index]() if values[index] is not None else None
        else:
            known[index] = combine([(c, known[p]) for c, p in terms])
    return [(known[r], known[i] if i is not None else None) for r, i in outputs]


def transposed_fourier(n, pairs, wanted):
    graph, inputs, outputs = fourier_graph(n)
    needed = set(wanted)
    for index, terms in enumerate(graph.terms):
        if any(p in needed for _, p in terms):
            needed.add(index)
    found = {index: [] for index in range(len(graph.terms))}
    for (r, i), (real, imag) in zip(outputs, pairs):
        found[r].append((1, real))
        if i is not None:
            found[i].append((1, imag))
    result = {}
    for index in reversed(range(len(graph.terms))):
        if index not in needed:
            continue
        value = combine(found[index])
        if index < n:
            result[index] = value
        for coef, parent in graph.terms[index]:
            found[parent].append((coef, value))
    return [result[index] for index in wanted]


def long_tables():
    b = np.arange(128)
    theta = 2 * np.pi * (b[None, :] * b[:, None] % 128) / 128
    cos, sin = np.cos(theta), np.sin(theta)
    first = np.concatenate([cos + sin, sin - cos], axis=1)
    second = np.concatenate([cos - sin, cos + sin], axis=1)[::-1]
    main = np.concatenate([first, second], axis=0) / math.sqrt(NX)
    angle = 2 * np.pi * (b[None, :] * (8 + 16 * b[:, None]) % NX) / NX
    edge = np.zeros((256, 256))
    edge[:128, :128] = cos + sin
    edge[128:, 128:] = np.cos(angle) + np.sin(angle)
    edge /= math.sqrt(NX)
    phase = 2 * np.pi * np.arange(8)[:, None] * b[None, :] / NX
    twist = np.stack([np.cos(phase), np.sin(phase)]).astype(np.float32)
    return main.astype(np.float32), edge.astype(np.float32), twist


def lane_rows():
    lane = np.arange(128)
    return lane // 32, lane % 32


def lane_band():
    lane = np.arange(128)
    return lane // 16 % 4, lane // 64 * 16 + lane % 16


def short_tables(lanes):
    group_in, index_in = lanes
    group_out, index_out = lane_rows()
    same = group_in[:, None] == group_out[None, :]
    theta = 2 * np.pi * (index_in[:, None] * index_out[None, :] % 32) / 32
    mirrored = 2 * np.pi * (index_in[:, None] * (31 - index_out)[None, :] % 32) / 32
    cos, sin = np.cos(theta), np.sin(theta)
    mcos, msin = np.cos(mirrored), np.sin(mirrored)
    top = np.concatenate([same * (cos + sin), same * (mcos - msin)], axis=1)
    bottom = np.concatenate([same * (sin - cos), same * (mcos + msin)], axis=1)
    main = np.concatenate([top, bottom], axis=0) / math.sqrt(NX)
    phase = 2 * np.pi * np.arange(33)[:, None] * index_in[None, :] / NX
    twist = np.stack([np.cos(phase), np.sin(phase)]).astype(np.float32)
    return main.astype(np.float32), twist


NN = (((1,), (0,)), ((), ()))
NT = (((1,), (1,)), ((), ()))


def split(x):
    high = x.astype(BF16)
    return high, (x - high.astype(F32)).astype(BF16)


def dot(a, b, dims):
    return lax.dot_general(a, b, dims, preferred_element_type=F32)


def product(x, table, dims):
    high, low = split(x)
    return dot(high, table[0], dims) + (dot(high, table[1], dims) + dot(low, table[0], dims))


def product_left(table, x, dims):
    high, low = split(x)
    return dot(table[0], high, dims) + (dot(table[1], high, dims) + dot(table[0], low, dims))


def long_forward(parts, twist, main, edge):
    spectrum = forward_fourier(16, [None if p is None else (lambda p=p: p) for p in parts])
    rows = [jnp.concatenate([spectrum[0][0], spectrum[8][0]], axis=1)]
    for k in range(1, 8):
        real, imag = spectrum[k]
        cos, sin = twist[0, k : k + 1, :], twist[1, k : k + 1, :]
        rows.append(jnp.concatenate([real * cos + imag * sin, imag * cos - real * sin], axis=1))
    size = rows[0].shape[0]
    data = jnp.concatenate(rows, axis=0)
    out = product_left(main, data, NT)
    special = product_left(edge, data[:128], NT)
    lanes = lax.broadcasted_iota(jnp.int32, (256, 128), 1)
    first = jnp.where(lanes < size, special, out[:, :128])
    if size == 16:
        return first
    return jnp.concatenate([first, out[:, 128:]], axis=1)


def long_backward(data, twist, main, edge, wanted):
    turned = data.T
    size = turned.shape[0] // 8
    out = product(turned, main, NN)
    special = product(turned[:size], edge, NN)
    pairs = [(special[:, :128], None)]
    for k in range(1, 8):
        real, imag = out[k * size : (k + 1) * size, :128], out[k * size : (k + 1) * size, 128:]
        cos, sin = twist[0, k : k + 1, :], twist[1, k : k + 1, :]
        pairs.append((real * cos - imag * sin, real * sin + imag * cos))
    pairs.append((special[:, 128:], None))
    return transposed_fourier(16, pairs, wanted)


def short_in(loaders, twist, store):
    spectrum = forward_fourier(64, loaders)
    for k in range(33):
        real, imag = spectrum[k]
        row = (k - 1) % 32 if k < 32 else 32
        if k == 0:
            store(row, real, jnp.zeros_like(real))
            continue
        cos, sin = twist[0, k : k + 1, :], twist[1, k : k + 1, :]
        if k == 32:
            store(row, real * cos, -(real * sin))
        else:
            store(row, real * cos + imag * sin, imag * cos - real * sin)


def short_out(load, twist, wanted):
    pairs = []
    for k in range(33):
        row = (k - 1) % 32 if k < 32 else 32
        real, imag = load(row)
        if k == 0:
            pairs.append((real, None))
            continue
        cos, sin = twist[0, k : k + 1, :], twist[1, k : k + 1, :]
        if k == 32:
            pairs.append((real * cos - imag * sin, None))
        else:
            pairs.append((real * cos - imag * sin, real * sin + imag * cos))
    return transposed_fourier(64, pairs, wanted)


def fold(tile):
    row = lax.broadcasted_iota(jnp.int32, (8, 128), 0)
    lane = lax.broadcasted_iota(jnp.int32, (8, 128), 1)
    other = pltpu.roll(pltpu.roll(tile, 4, 0), 64, 1)
    return jnp.where((row < 4) == (lane < 64), tile, other)


def kernel(
    right_hbm, time_hbm, col_hbm, lin_hbm, trow_hbm, tcol_hbm, u_hbm, v_hbm, noise_hbm, order_hbm,
    long_hbm, edge_hbm, ltw_hbm, short_hbm, shortp_hbm, stw_hbm, stwp_hbm,
    sol_ref, res_ref,
    right_ref, time_ref, col_ref, raw_ref, trow_ref, tcol_ref, u_ref, v_ref, noise_ref, order_ref,
    long_ref, edge_ref, ltw_ref, short_ref, shortp_ref, stw_ref, stwp_ref,
    long_tab, edge_tab, short_tab, shortp_tab, row_ref, turned, lin_ref,
    full_out, full_in, half_out, half_in, vis_out, vis_in, lin_in, red_out, red_in,
    kern_u, kern_t, kern_v, sky, mid, seen, resid,
    full_s, full_r, half_s, half_r, vis_s, vis_r, lin_s, lin_r, red_s, red_r, load_s,
):
    me = lax.axis_index("space")
    frame = lax.axis_index("tm")
    mine = (me // 16, me // 2 % 8, me % 2)

    def at(dx, dy, dc):
        return (mine[0] + dx) % 4 * 16 + (mine[1] + dy) % 8 * 2 + (mine[2] + dc) % 2

    def frame_peer(step):
        return (frame + step) % 8

    barrier = pltpu.get_barrier_semaphore()
    for offset in OFFSETS:
        pl.semaphore_signal(barrier, inc=1, device_id=(frame, at(*offset)), device_id_type=MESH)
    for step in range(1, 8):
        pl.semaphore_signal(barrier, inc=1, device_id=(frame_peer(step), me), device_id_type=MESH)

    loads = [
        pltpu.make_async_copy(src, dst, load_s.at[index])
        for index, (src, dst) in enumerate(
            (
                (right_hbm.at[0], right_ref),
                (time_hbm, time_ref),
                (col_hbm, col_ref),
                (ltw_hbm, ltw_ref),
                (long_hbm, long_ref),
                (edge_hbm, edge_ref),
                (lin_hbm.at[:, 0, :], raw_ref),
                (order_hbm, order_ref),
                (trow_hbm, trow_ref),
                (tcol_hbm, tcol_ref),
                (u_hbm.at[0], u_ref),
                (v_hbm.at[0], v_ref),
                (noise_hbm.at[0], noise_ref),
                (short_hbm, short_ref),
                (shortp_hbm, shortp_ref),
                (stw_hbm, stw_ref),
                (stwp_hbm, stwp_ref),
            )
        )
    ]
    for load in loads:
        load.start()

    def send_all(src, dst, send_sem, recv_sem):
        for offset in OFFSETS:
            other = at(*offset)
            pltpu.make_async_remote_copy(
                src_ref=src.at[other], dst_ref=dst.at[me], send_sem=send_sem, recv_sem=recv_sem,
                device_id=(frame, other), device_id_type=MESH,
            ).start()
        pltpu.make_async_copy(src.at[me], dst.at[me], recv_sem).start()

    def arrived(dst, recv_sem):
        pltpu.make_async_copy(dst, dst, recv_sem).wait()

    def sent(src, count, send_sem):
        part = src.at[pl.ds(0, count)]
        pltpu.make_async_copy(part, part, send_sem).wait()

    def reduce_peer(stage, step):
        if stage == 0:
            return (frame, at(step // 2, 0, step % 2))
        if stage == 1:
            return (frame, at(0, step, 0))
        return (frame_peer(step), me)

    def reduce_send(which, stage, value):
        index = which * 3 + stage
        red_out[index] = value
        for step in range(1, 8):
            pltpu.make_async_remote_copy(
                src_ref=red_out.at[index], dst_ref=red_in.at[index, step - 1],
                send_sem=red_s.at[index], recv_sem=red_r.at[index],
                device_id=reduce_peer(stage, step), device_id_type=MESH,
            ).start()

    def reduce_take(which, stage):
        index = which * 3 + stage
        arrived(red_in.at[index], red_r.at[index])
        return red_out[index] + jnp.sum(red_in[index], axis=0)

    def pack(*values):
        lane = lax.broadcasted_iota(jnp.int32, (8, 128), 1)
        row = lax.broadcasted_iota(jnp.int32, (8, 128), 0)
        total = jnp.zeros((8, 128), F32)
        for index, value in enumerate(values):
            total = total + jnp.where((lane == index) & (row == 0), value, 0.0)
        return total

    def unpack(tile, index):
        return tile[0:1, index : index + 1]

    def whole_sum(x):
        return jnp.sum(jnp.sum(x, axis=0, keepdims=True), axis=1, keepdims=True)

    def scale(a):
        return row_ref[...] * col_ref[:, 128 * a : 128 * (a + 1)]

    def scaled(ref, a):
        return ref[:, 128 * a : 128 * (a + 1)] * scale(a)

    def rows_to_columns(ref, n):
        out = long_forward([scaled(ref, a) for a in range(16)], ltw_ref, long_tab, edge_tab)
        for g in range(16):
            for h in range(2):
                for l in range(2):
                    full_out[n, 4 * g + 2 * h + l] = out[
                        128 * h + 8 * g : 128 * h + 8 * g + 8, 128 * l : 128 * (l + 1)
                    ]

    def send_full(n):
        send_all(full_out.at[n], full_in.at[n], full_s.at[n], full_r.at[n])

    def store_mid(row, real, imag):
        mid[8 * row : 8 * row + 8, 0:128] = real
        mid[8 * row : 8 * row + 8, 128:256] = imag

    def load_mid(row):
        return mid[8 * row : 8 * row + 8, 0:128], mid[8 * row : 8 * row + 8, 128:256]

    def through_sky(table_in, table_out):
        image = product(mid[...], table_in, NN) * sky[...]
        mid[...] = product(image, table_out, NT)

    def columns_to_band(n):
        arrived(full_in.at[n], full_r.at[n])
        short_in([lambda s=s: full_in[n, s] for s in range(64)], stw_ref, store_mid)
        through_sky(short_tab, shortp_tab)
        tiles = short_out(load_mid, stwp_ref, BAND_TILES)
        for s, tile in enumerate(tiles):
            folded = fold(tile)
            half_out[n, 2 * s] = folded[0:4]
            half_out[n, 2 * s + 1] = folded[4:8]
        send_all(half_out.at[n], half_in.at[n], half_s.at[n], half_r.at[n])

    def pair_of(n, index):
        return fold(jnp.concatenate([half_in[n, 2 * index], half_in[n, 2 * index + 1]], axis=0))

    def band_to_grid(n):
        arrived(half_in.at[n], half_r.at[n])
        rows = [pair_of(n, 2 * g + h) for h in range(2) for g in range(16)]
        parts = long_backward(
            jnp.concatenate(rows, axis=0), ltw_ref, long_tab, edge_tab, BAND_PARTS
        )
        return jnp.concatenate(parts, axis=0)

    def grid_to_band(grid, n):
        parts = [None] * 16
        for index, a in enumerate(BAND_PARTS):
            parts[a] = grid[BAND * index : BAND * (index + 1)]
        out = long_forward(parts, ltw_ref, long_tab, edge_tab)
        for g in range(16):
            for h in range(2):
                folded = fold(out[128 * h + 8 * g : 128 * h + 8 * g + 8])
                half_out[n, 4 * g + 2 * h] = folded[0:4]
                half_out[n, 4 * g + 2 * h + 1] = folded[4:8]
        send_all(half_out.at[n], half_in.at[n], half_s.at[n], half_r.at[n])

    def band_to_columns(n, m):
        arrived(half_in.at[n], half_r.at[n])
        loaders = [None] * 64
        for index, s in enumerate(BAND_TILES):
            loaders[s] = lambda index=index: pair_of(n, index)
        short_in(loaders, stwp_ref, store_mid)
        through_sky(shortp_tab, short_tab)
        tiles = short_out(load_mid, stw_ref, list(range(64)))
        for s, tile in enumerate(tiles):
            full_out[m, s] = tile
        send_full(m)

    def columns_to_rows(n):
        arrived(full_in.at[n], full_r.at[n])
        data = jnp.concatenate(
            [
                jnp.concatenate(
                    [full_in[n, 4 * g + 2 * h + l] for h in range(2) for g in range(16)], axis=0
                )
                for l in range(2)
            ],
            axis=1,
        )
        parts = long_backward(data, ltw_ref, long_tab, edge_tab, list(range(16)))
        return [part * scale(a) for a, part in enumerate(parts)]

    def measure(grid, factor, first):
        tiles = [grid[BAND * k : BAND * (k + 1)] for k in range(8)]
        zero = jnp.zeros((BAND, 128), BF16)

        def step(start, carry):
            total, sums = carry[0], list(carry[1:])
            for c in [start * UNROLL + index for index in range(UNROLL)]:
                table = kern_u[c]
                weights = kern_v[c]
                columns, rows = [], []
                for block in (2 * c, 2 * c + 1):
                    column = vis_in[block, 3:4]
                    tile = tiles[0]
                    for k in range(1, 8):
                        tile = jnp.where(column == float(k), tiles[k], tile)
                    high, low = split(tile)
                    columns.append(column)
                    rows.append(jnp.concatenate([high, high], axis=1))
                    rows.append(jnp.concatenate([low, zero], axis=1))
                both = dot(jnp.concatenate(rows, axis=0), table, NN)
                picked = jnp.concatenate(
                    [both[0:16, :128] + both[16:32, :128], both[32:48, 128:] + both[48:64, 128:]],
                    axis=1,
                )
                values = jnp.sum(picked * weights, axis=0, keepdims=True)
                if first:
                    seen[c] = jnp.broadcast_to(values, (8, 256))
                else:
                    values = values + factor * seen[c][0:1]
                noise = jnp.concatenate([vis_in[2 * c, 2:3], vis_in[2 * c + 1, 2:3]], axis=1)
                weighed = noise * values
                total = total + weighed * values
                up, down = split(weights * weighed)
                spread = jnp.concatenate(
                    [
                        jnp.concatenate([up[:, :128], zero], axis=1),
                        jnp.concatenate([down[:, :128], zero], axis=1),
                        jnp.concatenate([zero, up[:, 128:]], axis=1),
                        jnp.concatenate([zero, down[:, 128:]], axis=1),
                    ],
                    axis=0,
                )
                back = dot(spread, kern_t[c], NN)
                for index, column in enumerate(columns):
                    high = back[32 * index : 32 * index + 16]
                    low = back[32 * index + 16 : 32 * index + 32]
                    tile = high[:, :128] + (high[:, 128:] + low[:, :128])
                    for k in range(8):
                        sums[k] = sums[k] + jnp.where(column == float(k), tile, 0.0)
            return (total, *sums)

        empty = [jnp.zeros((1, 256), F32)] + [jnp.zeros((BAND, 128), F32)] * 8
        total, *sums = lax.fori_loop(0, CHUNKS // UNROLL, step, tuple(empty))
        return jnp.concatenate(sums, axis=0), whole_sum(total)

    def exact(picker, values):
        high = values.astype(BF16)
        rest = values - high.astype(F32)
        middle = rest.astype(BF16)
        low = (rest - middle.astype(F32)).astype(BF16)
        return (dot(picker, high, NN) + dot(picker, middle, NN)) + dot(picker, low, NN)

    def both_parts(table, parts):
        parts[0], parts[1] = split(table[...])

    for load in loads[:6]:
        load.wait()
    columns = lax.broadcasted_iota(jnp.int32, (ROWS, NX), 1)
    rows = lax.broadcasted_iota(jnp.int32, (ROWS, NX), 0)
    amp_rows = jnp.sum(
        jnp.where(columns == me * ROWS + rows, col_ref[...], 0.0), axis=1, keepdims=True
    )
    row_ref[...] = jnp.broadcast_to(amp_rows * time_ref[...], (ROWS, 128))
    both_parts(long_ref, long_tab)
    both_parts(edge_ref, edge_tab)
    rows_to_columns(right_ref, 0)
    right_sum = whole_sum(right_ref[...] * right_ref[...])

    for load in loads[8:13]:
        load.wait()
    chosen = lax.broadcasted_iota(jnp.int32, (64, 64), 0) == trow_ref[...]
    picker = chosen.astype(BF16)
    columns = jnp.sum(
        jnp.where(chosen, tcol_ref[...].astype(F32), 0.0), axis=1, keepdims=True
    )
    for index, ref in enumerate((u_ref, v_ref, noise_ref)):
        vis_out[:, index, :] = exact(picker, ref[...])
    vis_out[:, 3, :] = jnp.broadcast_to(columns, (64, 128))

    for load in loads[6:8]:
        load.wait()
    ordered = exact(order_ref[...].astype(BF16), raw_ref[...])
    for c in range(16):
        turned[128 * c : 128 * (c + 1), 0:32] = ordered[:, 128 * c : 128 * (c + 1)].T
    for a in range(16):
        four = jnp.concatenate(
            [turned[pl.ds(4 * a + r, 32, stride=64), 0:32] for r in range(4)], axis=1
        )
        back = four.T
        for r in range(4):
            tile = jnp.concatenate(
                [back[32 * r + 8 * k : 32 * r + 8 * k + 8] for k in range(4)], axis=1
            )
            for hl in range(4):
                lin_ref[hl, 4 * a + r] = tile[2 * hl : 2 * hl + 2]

    for load in loads[13:]:
        load.wait()
    both_parts(short_ref, short_tab)
    both_parts(shortp_ref, shortp_tab)
    pl.semaphore_wait(barrier, len(OFFSETS) + 7)
    send_full(0)
    place = me % 4
    for step in range(1, 4):
        target = (place + step) % 4
        pltpu.make_async_remote_copy(
            src_ref=lin_ref.at[target], dst_ref=lin_in.at[place], send_sem=lin_s, recv_sem=lin_r,
            device_id=(frame, me - place + target), device_id_type=MESH,
        ).start()
    pltpu.make_async_copy(lin_ref.at[place], lin_in.at[place], lin_r).start()
    send_all(vis_out, vis_in, vis_s, vis_r)

    def build(c, carry):
        def pair(index):
            return jnp.concatenate(
                [vis_in[2 * c, index : index + 1], vis_in[2 * c + 1, index : index + 1]], axis=1
            )

        cells = lax.broadcasted_iota(jnp.int32, (128, 256), 0).astype(F32)
        away = (cells - pair(0)) * (8.0 / 128)
        values = jnp.exp(-0.5 * (away * away))
        high, low = split(values)
        kern_u[c, 0:128] = high
        kern_u[c, 128:256] = low
        high, low = split(values.T)
        kern_t[c, :, 0:128] = high
        kern_t[c, :, 128:256] = low
        cells = lax.broadcasted_iota(jnp.int32, (16, 256), 0).astype(F32)
        away = (cells - pair(1)) * (4.0 / 16)
        kern_v[c] = jnp.exp(-0.5 * (away * away))
        return carry

    arrived(lin_in, lin_r)

    def sky_tile(k):
        return jnp.concatenate([lin_in[r, k] for r in range(4)], axis=0)

    for k in range(1, 32):
        sky[8 * (k - 1) : 8 * k, 0:128] = sky_tile(k)
        sky[8 * (k - 1) : 8 * k, 128:256] = sky_tile(64 - k)
    sky[248:256, 0:128] = sky_tile(0)
    sky[256:264, 0:128] = sky_tile(32)
    sky[248:264, 128:256] = jnp.zeros((16, 128), F32)

    columns_to_band(0)
    arrived(vis_in, vis_r)
    lax.fori_loop(0, CHUNKS, build, 0, unroll=2)
    grid, weight_sum = measure(band_to_grid(0), None, True)
    reduce_send(0, 0, pack(right_sum, weight_sum))
    grid_to_band(grid, 1)
    reduce_send(0, 1, reduce_take(0, 0))
    band_to_columns(1, 1)
    reduce_send(0, 2, reduce_take(0, 1))
    harmonic = columns_to_rows(1)
    sums = reduce_take(0, 2)
    norm_zero = unpack(sums, 0)
    step_zero = norm_zero / (norm_zero + unpack(sums, 1))
    square = jnp.zeros((32, 128), F32)
    cross = jnp.zeros((32, 128), F32)
    for a in range(16):
        lanes = slice(128 * a, 128 * (a + 1))
        before = right_ref[:, lanes]
        after = before - step_zero * (before + harmonic[a])
        resid[:, lanes] = after
        square = square + after * after
        cross = cross + after * before

    reduce_send(1, 0, pack(whole_sum(square), whole_sum(cross)))
    rows_to_columns(resid, 2)
    send_full(2)
    reduce_send(1, 1, reduce_take(1, 0))
    columns_to_band(2)
    reduce_send(1, 2, reduce_take(1, 1))
    grid = band_to_grid(2)
    sums = reduce_take(1, 2)
    norm_one = unpack(sums, 0)
    growth = norm_one / norm_zero
    squared = norm_one + 2.0 * growth * unpack(sums, 1) + growth * growth * norm_zero
    grid, weight_sum = measure(grid, growth, False)
    reduce_send(2, 0, pack(weight_sum))
    grid_to_band(grid, 3)
    reduce_send(2, 1, reduce_take(2, 0))
    band_to_columns(3, 3)
    reduce_send(2, 2, reduce_take(2, 1))
    harmonic = columns_to_rows(3)
    sums = reduce_take(2, 2)
    step_one = norm_one / (squared + unpack(sums, 0))
    for a in range(16):
        lanes = slice(128 * a, 128 * (a + 1))
        before = right_ref[:, lanes]
        after = resid[:, lanes]
        direction = after + growth * before
        sol_ref[:, lanes] = step_zero * before + step_one * direction
        res_ref[:, lanes] = after - step_one * (direction + harmonic[a])

    for n in range(4):
        sent(full_out.at[n], 63, full_s.at[n])
        sent(half_out.at[n], 63, half_s.at[n])
    sent(vis_out, 63, vis_s)
    sent(lin_ref, 3, lin_s)
    for index in range(9):
        sent(red_in.at[index], 7, red_s.at[index])


def shards(
    right_side, amp_time, amp_space, lin_sky, tile_row, tile_col, u_frac, v_frac, noise_weight
):
    order = np.zeros((32, 32))
    for row, (kappa, half, left, k2) in enumerate(np.ndindex(4, 2, 2, 2)):
        index = 4 * left + kappa
        k1 = index if half == 0 else 8 if index == 0 else 16 - index
        order[row, 16 * k2 + k1] = 1.0
    long_main, long_edge, long_twist = long_tables()
    short_main, short_twist = short_tables(lane_rows())
    band_main, band_twist = short_tables(lane_band())
    operands = (
        right_side,
        amp_time.reshape(1, 1),
        amp_space.reshape(1, NX),
        lin_sky,
        tile_row,
        tile_col,
        u_frac,
        v_frac,
        noise_weight,
        jnp.asarray(order, F32),
        *(
            jnp.asarray(t)
            for t in (
                long_main, long_edge, long_twist, short_main, band_main, short_twist, band_twist,
            )
        ),
    )
    vmem = pl.BlockSpec(memory_space=pltpu.VMEM)
    dma = pltpu.SemaphoreType.DMA
    outs = pl.pallas_call(
        kernel,
        out_shape=[jax.ShapeDtypeStruct((ROWS, NX), F32)] * 2,
        in_specs=[pl.BlockSpec(memory_space=pltpu.MemorySpace.HBM)] * len(operands),
        out_specs=[vmem] * 2,
        scratch_shapes=[
            pltpu.VMEM((ROWS, NX), F32),
            *(pltpu.VMEM(o.shape, o.dtype) for o in operands[1:3]),
            pltpu.VMEM((ROWS, NX), F32),
            *(pltpu.VMEM(o.shape, o.dtype) for o in operands[4:6]),
            *[pltpu.VMEM((BLOCKS, 128), F32)] * 3,
            *(pltpu.VMEM(o.shape, o.dtype) for o in operands[9:]),
            *[pltpu.VMEM((2, 256, 256), BF16)] * 4,
            pltpu.VMEM((ROWS, 128), F32),
            pltpu.VMEM((NX, 128), F32),
            pltpu.VMEM((4, 64, 2, 128), F32),
            pltpu.VMEM((4, 64, 8, 128), F32),
            pltpu.VMEM((4, 64, 8, 128), F32),
            pltpu.VMEM((4, 64, 4, 128), F32),
            pltpu.VMEM((4, 64, 4, 128), F32),
            pltpu.VMEM((64, 4, 128), F32),
            pltpu.VMEM((64, 4, 128), F32),
            pltpu.VMEM((4, 64, 2, 128), F32),
            pltpu.VMEM((9, 8, 128), F32),
            pltpu.VMEM((9, 7, 8, 128), F32),
            pltpu.VMEM((CHUNKS, 256, 256), BF16),
            pltpu.VMEM((CHUNKS, 256, 256), BF16),
            pltpu.VMEM((CHUNKS, BAND, 256), F32),
            pltpu.VMEM((264, 256), F32),
            pltpu.VMEM((264, 256), F32),
            pltpu.VMEM((CHUNKS, 8, 256), F32),
            pltpu.VMEM((ROWS, NX), F32),
            dma((4,)), dma((4,)), dma((4,)), dma((4,)),
            dma, dma, dma, dma,
            dma((9,)), dma((9,)), dma((17,)),
        ],
        compiler_params=pltpu.CompilerParams(
            collective_id=0, has_side_effects=True, vmem_limit_bytes=63 * 1024 * 1024
        ),
    )(*operands)
    return tuple(out.reshape(1, ROWS, NX) for out in outs)


def solution(mesh):
    in_specs = (
        P("tm", "space", None),
        P("tm"),
        P(),
        P("space", "tm", None),
        P("tm", "space"),
        P("tm", "space"),
        P("tm", "space", None),
        P("tm", "space", None),
        P("tm", "space", None),
    )
    out_specs = (P("tm", "space", None), P("tm", "space", None))
    return jax.shard_map(shards, mesh=mesh, in_specs=in_specs, out_specs=out_specs, check_vma=False)
```

```python
import functools
import math

import jax
import jax.numpy as jnp
import numpy as np
from jax import lax
from jax.experimental import pallas as pl
from jax.experimental.pallas import tpu as pltpu
from jax.sharding import PartitionSpec as P

NX = 2048
GROUPS = 64
ROWS = 32
BAND = 16
BLOCKS = 64
CHUNKS = 32
UNROLL = 16
MESH = pl.DeviceIdType.MESH
F32 = jnp.float32
BF16 = jnp.bfloat16

BAND_TILES = list(range(16)) + list(range(48, 64))
BAND_PARTS = [0, 1, 2, 3, 12, 13, 14, 15]

ORDER = [
    40, 41, 42, 25, 57, 38, 39, 43, 24, 56, 59, 37, 44, 27, 9, 36,
    23, 22, 8, 45, 26, 54, 58, 55, 10, 7, 21, 34, 47, 46, 29, 35,
    28, 60, 53, 20, 52, 11, 6, 61, 50, 32, 31, 30, 5, 19, 13, 51,
    12, 18, 63, 33, 4, 62, 16, 49, 15, 2, 3, 14, 17, 48, 1,
]
OFFSETS = [(code // 16, code // 2 % 8, code % 2) for code in ORDER]


class Graph:
    def __init__(self):
        self.terms = []

    def node(self, *terms):
        self.terms.append(terms)
        return len(self.terms) - 1


def real_fourier(graph, inputs):
    n = len(inputs)
    if n == 1:
        return [(inputs[0], None)]
    if n == 2:
        a, b = inputs
        return [(graph.node((1, a), (1, b)), None), (graph.node((1, a), (-1, b)), None)]
    even = real_fourier(graph, inputs[0::2])
    odd = real_fourier(graph, inputs[1::2])
    out = [None] * (n // 2 + 1)
    e, o = even[0][0], odd[0][0]
    out[0] = (graph.node((1, e), (1, o)), None)
    out[n // 2] = (graph.node((1, e), (-1, o)), None)
    for k in range(1, n // 4):
        cos, sin = math.cos(2 * math.pi * k / n), math.sin(2 * math.pi * k / n)
        er, ei = even[k]
        ore, oim = odd[k]
        tr = graph.node((cos, ore), (sin, oim))
        ti = graph.node((cos, oim), (-sin, ore))
        out[k] = (graph.node((1, er), (1, tr)), graph.node((1, ei), (1, ti)))
        out[n // 2 - k] = (graph.node((1, er), (-1, tr)), graph.node((1, ti), (-1, ei)))
    e, o = even[n // 4][0], odd[n // 4][0]
    out[n // 4] = (e, graph.node((-1, o)))
    return out


def fourier_graph(n):
    graph = Graph()
    inputs = [graph.node() for _ in range(n)]
    return graph, inputs, real_fourier(graph, inputs)


def combine(terms):
    terms = [(c, v) for c, v in terms if v is not None]
    if not terms:
        return None
    terms.sort(key=lambda t: t[0] < 0)
    coef, total = terms[0]
    if coef == -1:
        total = -total
    elif coef != 1:
        total = total * coef
    for coef, value in terms[1:]:
        if coef == 1:
            total = total + value
        elif coef == -1:
            total = total - value
        elif coef < 0:
            total = total - value * (-coef)
        else:
            total = total + value * coef
    return total


def forward_fourier(n, values):
    graph, inputs, outputs = fourier_graph(n)
    known = {}
    for index, terms in enumerate(graph.terms):
        if index < n:
            known[index] = values[index]() if values[index] is not None else None
        else:
            known[index] = combine([(c, known[p]) for c, p in terms])
    return [(known[r], known[i] if i is not None else None) for r, i in outputs]


def transposed_fourier(n, pairs, wanted):
    graph, inputs, outputs = fourier_graph(n)
    needed = set(wanted)
    for index, terms in enumerate(graph.terms):
        if any(p in needed for _, p in terms):
            needed.add(index)
    found = {index: [] for index in range(len(graph.terms))}
    for (r, i), (real, imag) in zip(outputs, pairs):
        found[r].append((1, real))
        if i is not None:
            found[i].append((1, imag))
    result = {}
    for index in reversed(range(len(graph.terms))):
        if index not in needed:
            continue
        value = combine(found[index])
        if index < n:
            result[index] = value
        for coef, parent in graph.terms[index]:
            found[parent].append((coef, value))
    return [result[index] for index in wanted]


def long_tables():
    b = np.arange(128)
    theta = 2 * np.pi * (b[None, :] * b[:, None] % 128) / 128
    cos, sin = np.cos(theta), np.sin(theta)
    first = np.concatenate([cos + sin, sin - cos], axis=1)
    second = np.concatenate([cos - sin, cos + sin], axis=1)[::-1]
    main = np.concatenate([first, second], axis=0) / math.sqrt(NX)
    angle = 2 * np.pi * (b[None, :] * (8 + 16 * b[:, None]) % NX) / NX
    edge = np.zeros((256, 256))
    edge[:128, :128] = cos + sin
    edge[128:, 128:] = np.cos(angle) + np.sin(angle)
    edge /= math.sqrt(NX)
    phase = 2 * np.pi * np.arange(8)[:, None] * b[None, :] / NX
    twist = np.stack([np.cos(phase), np.sin(phase)]).astype(np.float32)
    return main.astype(np.float32), edge.astype(np.float32), twist


def lane_rows():
    lane = np.arange(128)
    return lane // 32, lane % 32


def lane_band():
    lane = np.arange(128)
    return lane // 16 % 4, lane // 64 * 16 + lane % 16


def short_tables(lanes):
    group_in, index_in = lanes
    group_out, index_out = lane_rows()
    same = group_in[:, None] == group_out[None, :]
    theta = 2 * np.pi * (index_in[:, None] * index_out[None, :] % 32) / 32
    mirrored = 2 * np.pi * (index_in[:, None] * (31 - index_out)[None, :] % 32) / 32
    cos, sin = np.cos(theta), np.sin(theta)
    mcos, msin = np.cos(mirrored), np.sin(mirrored)
    top = np.concatenate([same * (cos + sin), same * (mcos - msin)], axis=1)
    bottom = np.concatenate([same * (sin - cos), same * (mcos + msin)], axis=1)
    main = np.concatenate([top, bottom], axis=0) / math.sqrt(NX)
    phase = 2 * np.pi * np.arange(33)[:, None] * index_in[None, :] / NX
    twist = np.stack([np.cos(phase), np.sin(phase)]).astype(np.float32)
    return main.astype(np.float32), twist


NN = (((1,), (0,)), ((), ()))
NT = (((1,), (1,)), ((), ()))


def split(x):
    high = x.astype(BF16)
    return high, (x - high.astype(F32)).astype(BF16)


def dot(a, b, dims):
    return lax.dot_general(a, b, dims, preferred_element_type=F32)


def product(x, table, dims):
    high, low = split(x)
    return dot(high, table[0], dims) + (dot(high, table[1], dims) + dot(low, table[0], dims))


def product_left(table, x, dims):
    high, low = split(x)
    return dot(table[0], high, dims) + (dot(table[1], high, dims) + dot(table[0], low, dims))


def long_forward(parts, twist, main, edge):
    spectrum = forward_fourier(16, [None if p is None else (lambda p=p: p) for p in parts])
    rows = [jnp.concatenate([spectrum[0][0], spectrum[8][0]], axis=1)]
    for k in range(1, 8):
        real, imag = spectrum[k]
        cos, sin = twist[0, k : k + 1, :], twist[1, k : k + 1, :]
        rows.append(jnp.concatenate([real * cos + imag * sin, imag * cos - real * sin], axis=1))
    size = rows[0].shape[0]
    data = jnp.concatenate(rows, axis=0)
    out = product_left(main, data, NT)
    special = product_left(edge, data[:128], NT)
    lanes = lax.broadcasted_iota(jnp.int32, (256, 128), 1)
    first = jnp.where(lanes < size, special, out[:, :128])
    if size == 16:
        return first
    return jnp.concatenate([first, out[:, 128:]], axis=1)


def long_backward(data, twist, main, edge, wanted):
    turned = data.T
    size = turned.shape[0] // 8
    out = product(turned, main, NN)
    special = product(turned[:size], edge, NN)
    pairs = [(special[:, :128], None)]
    for k in range(1, 8):
        real, imag = out[k * size : (k + 1) * size, :128], out[k * size : (k + 1) * size, 128:]
        cos, sin = twist[0, k : k + 1, :], twist[1, k : k + 1, :]
        pairs.append((real * cos - imag * sin, real * sin + imag * cos))
    pairs.append((special[:, 128:], None))
    return transposed_fourier(16, pairs, wanted)


def short_in(loaders, twist, store):
    spectrum = forward_fourier(64, loaders)
    for k in range(33):
        real, imag = spectrum[k]
        row = (k - 1) % 32 if k < 32 else 32
        if k == 0:
            store(row, real, jnp.zeros_like(real))
            continue
        cos, sin = twist[0, k : k + 1, :], twist[1, k : k + 1, :]
        if k == 32:
            store(row, real * cos, -(real * sin))
        else:
            store(row, real * cos + imag * sin, imag * cos - real * sin)


def short_out(load, twist, wanted):
    pairs = []
    for k in range(33):
        row = (k - 1) % 32 if k < 32 else 32
        real, imag = load(row)
        if k == 0:
            pairs.append((real, None))
            continue
        cos, sin = twist[0, k : k + 1, :], twist[1, k : k + 1, :]
        if k == 32:
            pairs.append((real * cos - imag * sin, None))
        else:
            pairs.append((real * cos - imag * sin, real * sin + imag * cos))
    return transposed_fourier(64, pairs, wanted)


def fold(tile):
    row = lax.broadcasted_iota(jnp.int32, (8, 128), 0)
    lane = lax.broadcasted_iota(jnp.int32, (8, 128), 1)
    other = pltpu.roll(pltpu.roll(tile, 4, 0), 64, 1)
    return jnp.where((row < 4) == (lane < 64), tile, other)


def kernel(
    right_hbm, time_hbm, col_hbm, lin_hbm, trow_hbm, tcol_hbm, u_hbm, v_hbm, noise_hbm, order_hbm,
    long_hbm, edge_hbm, ltw_hbm, short_hbm, shortp_hbm, stw_hbm, stwp_hbm,
    sol_ref, res_ref,
    right_ref, time_ref, col_ref, raw_ref, trow_ref, tcol_ref, u_ref, v_ref, noise_ref, order_ref,
    long_ref, edge_ref, ltw_ref, short_ref, shortp_ref, stw_ref, stwp_ref,
    long_tab, edge_tab, short_tab, shortp_tab, row_ref, turned, lin_ref,
    full_out, full_in, half_out, half_in, vis_out, vis_in, lin_in, red_out, red_in,
    kern_u, kern_t, kern_v, sky, mid, seen, resid,
    full_s, full_r, half_s, half_r, vis_s, vis_r, lin_s, lin_r, red_s, red_r, load_s,
):
    me = lax.axis_index("space")
    frame = lax.axis_index("tm")
    mine = (me // 16, me // 2 % 8, me % 2)

    def at(dx, dy, dc):
        return (mine[0] + dx) % 4 * 16 + (mine[1] + dy) % 8 * 2 + (mine[2] + dc) % 2

    def frame_peer(step):
        return (frame + step) % 8

    barrier = pltpu.get_barrier_semaphore()
    for offset in OFFSETS:
        pl.semaphore_signal(barrier, inc=1, device_id=(frame, at(*offset)), device_id_type=MESH)
    for step in range(1, 8):
        pl.semaphore_signal(barrier, inc=1, device_id=(frame_peer(step), me), device_id_type=MESH)

    loads = [
        pltpu.make_async_copy(src, dst, load_s.at[index])
        for index, (src, dst) in enumerate(
            (
                (right_hbm.at[0], right_ref),
                (time_hbm, time_ref),
                (col_hbm, col_ref),
                (ltw_hbm, ltw_ref),
                (long_hbm, long_ref),
                (edge_hbm, edge_ref),
                (lin_hbm.at[:, 0, :], raw_ref),
                (order_hbm, order_ref),
                (trow_hbm, trow_ref),
                (tcol_hbm, tcol_ref),
                (u_hbm.at[0], u_ref),
                (v_hbm.at[0], v_ref),
                (noise_hbm.at[0], noise_ref),
                (short_hbm, short_ref),
                (shortp_hbm, shortp_ref),
                (stw_hbm, stw_ref),
                (stwp_hbm, stwp_ref),
            )
        )
    ]
    for load in loads:
        load.start()

    def send_all(src, dst, send_sem, recv_sem):
        for offset in OFFSETS:
            other = at(*offset)
            pltpu.make_async_remote_copy(
                src_ref=src.at[other], dst_ref=dst.at[me], send_sem=send_sem, recv_sem=recv_sem,
                device_id=(frame, other), device_id_type=MESH,
            ).start()
        pltpu.make_async_copy(src.at[me], dst.at[me], recv_sem).start()

    def arrived(dst, recv_sem):
        pltpu.make_async_copy(dst, dst, recv_sem).wait()

    def sent(src, count, send_sem):
        part = src.at[pl.ds(0, count)]
        pltpu.make_async_copy(part, part, send_sem).wait()

    def reduce_peer(stage, step):
        if stage == 0:
            return (frame, at(step // 2, 0, step % 2))
        if stage == 1:
            return (frame, at(0, step, 0))
        return (frame_peer(step), me)

    def reduce_send(which, stage, value):
        index = which * 3 + stage
        red_out[index] = value
        for step in range(1, 8):
            pltpu.make_async_remote_copy(
                src_ref=red_out.at[index], dst_ref=red_in.at[index, step - 1],
                send_sem=red_s.at[index], recv_sem=red_r.at[index],
                device_id=reduce_peer(stage, step), device_id_type=MESH,
            ).start()

    def reduce_take(which, stage):
        index = which * 3 + stage
        arrived(red_in.at[index], red_r.at[index])
        return red_out[index] + jnp.sum(red_in[index], axis=0)

    def pack(*values):
        lane = lax.broadcasted_iota(jnp.int32, (8, 128), 1)
        row = lax.broadcasted_iota(jnp.int32, (8, 128), 0)
        total = jnp.zeros((8, 128), F32)
        for index, value in enumerate(values):
            total = total + jnp.where((lane == index) & (row == 0), value, 0.0)
        return total

    def unpack(tile, index):
        return tile[0:1, index : index + 1]

    def whole_sum(x):
        return jnp.sum(jnp.sum(x, axis=0, keepdims=True), axis=1, keepdims=True)

    def scale(a):
        return row_ref[...] * col_ref[:, 128 * a : 128 * (a + 1)]

    def scaled(ref, a):
        return ref[:, 128 * a : 128 * (a + 1)] * scale(a)

    def rows_to_columns(ref, n):
        out = long_forward([scaled(ref, a) for a in range(16)], ltw_ref, long_tab, edge_tab)
        for g in range(16):
            for h in range(2):
                for l in range(2):
                    full_out[n, 4 * g + 2 * h + l] = out[
                        128 * h + 8 * g : 128 * h + 8 * g + 8, 128 * l : 128 * (l + 1)
                    ]

    def send_full(n):
        send_all(full_out.at[n], full_in.at[n], full_s.at[n], full_r.at[n])

    def store_mid(row, real, imag):
        mid[8 * row : 8 * row + 8, 0:128] = real
        mid[8 * row : 8 * row + 8, 128:256] = imag

    def load_mid(row):
        return mid[8 * row : 8 * row + 8, 0:128], mid[8 * row : 8 * row + 8, 128:256]

    def through_sky(table_in, table_out):
        image = product(mid[...], table_in, NN) * sky[...]
        mid[...] = product(image, table_out, NT)

    def columns_to_band(n):
        arrived(full_in.at[n], full_r.at[n])
        short_in([lambda s=s: full_in[n, s] for s in range(64)], stw_ref, store_mid)
        through_sky(short_tab, shortp_tab)
        tiles = short_out(load_mid, stwp_ref, BAND_TILES)
        for s, tile in enumerate(tiles):
            folded = fold(tile)
            half_out[n, 2 * s] = folded[0:4]
            half_out[n, 2 * s + 1] = folded[4:8]
        send_all(half_out.at[n], half_in.at[n], half_s.at[n], half_r.at[n])

    def pair_of(n, index):
        return fold(jnp.concatenate([half_in[n, 2 * index], half_in[n, 2 * index + 1]], axis=0))

    def band_to_grid(n):
        arrived(half_in.at[n], half_r.at[n])
        rows = [pair_of(n, 2 * g + h) for h in range(2) for g in range(16)]
        parts = long_backward(
            jnp.concatenate(rows, axis=0), ltw_ref, long_tab, edge_tab, BAND_PARTS
        )
        return jnp.concatenate(parts, axis=0)

    def grid_to_band(grid, n):
        parts = [None] * 16
        for index, a in enumerate(BAND_PARTS):
            parts[a] = grid[BAND * index : BAND * (index + 1)]
        out = long_forward(parts, ltw_ref, long_tab, edge_tab)
        for g in range(16):
            for h in range(2):
                folded = fold(out[128 * h + 8 * g : 128 * h + 8 * g + 8])
                half_out[n, 4 * g + 2 * h] = folded[0:4]
                half_out[n, 4 * g + 2 * h + 1] = folded[4:8]
        send_all(half_out.at[n], half_in.at[n], half_s.at[n], half_r.at[n])

    def band_to_columns(n, m):
        arrived(half_in.at[n], half_r.at[n])
        loaders = [None] * 64
        for index, s in enumerate(BAND_TILES):
            loaders[s] = lambda index=index: pair_of(n, index)
        short_in(loaders, stwp_ref, store_mid)
        through_sky(shortp_tab, short_tab)
        tiles = short_out(load_mid, stw_ref, list(range(64)))
        for s, tile in enumerate(tiles):
            full_out[m, s] = tile
        send_full(m)

    def columns_to_rows(n):
        arrived(full_in.at[n], full_r.at[n])
        data = jnp.concatenate(
            [
                jnp.concatenate(
                    [full_in[n, 4 * g + 2 * h + l] for h in range(2) for g in range(16)], axis=0
                )
                for l in range(2)
            ],
            axis=1,
        )
        parts = long_backward(data, ltw_ref, long_tab, edge_tab, list(range(16)))
        return [part * scale(a) for a, part in enumerate(parts)]

    def measure(grid, factor, first):
        tiles = [grid[BAND * k : BAND * (k + 1)] for k in range(8)]
        zero = jnp.zeros((BAND, 128), BF16)

        def step(start, carry):
            total, sums = carry[0], list(carry[1:])
            for c in [start * UNROLL + index for index in range(UNROLL)]:
                table = kern_u[c]
                weights = kern_v[c]
                columns, rows = [], []
                for block in (2 * c, 2 * c + 1):
                    column = vis_in[block, 3:4]
                    tile = tiles[0]
                    for k in range(1, 8):
                        tile = jnp.where(column == float(k), tiles[k], tile)
                    high, low = split(tile)
                    columns.append(column)
                    rows.append(jnp.concatenate([high, high], axis=1))
                    rows.append(jnp.concatenate([low, zero], axis=1))
                both = dot(jnp.concatenate(rows, axis=0), table, NN)
                picked = jnp.concatenate(
                    [both[0:16, :128] + both[16:32, :128], both[32:48, 128:] + both[48:64, 128:]],
                    axis=1,
                )
                values = jnp.sum(picked * weights, axis=0, keepdims=True)
                if first:
                    seen[c] = jnp.broadcast_to(values, (8, 256))
                else:
                    values = values + factor * seen[c][0:1]
                noise = jnp.concatenate([vis_in[2 * c, 2:3], vis_in[2 * c + 1, 2:3]], axis=1)
                weighed = noise * values
                total = total + weighed * values
                up, down = split(weights * weighed)
                spread = jnp.concatenate(
                    [
                        jnp.concatenate([up[:, :128], zero], axis=1),
                        jnp.concatenate([down[:, :128], zero], axis=1),
                        jnp.concatenate([zero, up[:, 128:]], axis=1),
                        jnp.concatenate([zero, down[:, 128:]], axis=1),
                    ],
                    axis=0,
                )
                back = dot(spread, kern_t[c], NN)
                for index, column in enumerate(columns):
                    high = back[32 * index : 32 * index + 16]
                    low = back[32 * index + 16 : 32 * index + 32]
                    tile = high[:, :128] + (high[:, 128:] + low[:, :128])
                    for k in range(8):
                        sums[k] = sums[k] + jnp.where(column == float(k), tile, 0.0)
            return (total, *sums)

        empty = [jnp.zeros((1, 256), F32)] + [jnp.zeros((BAND, 128), F32)] * 8
        total, *sums = lax.fori_loop(0, CHUNKS // UNROLL, step, tuple(empty))
        return jnp.concatenate(sums, axis=0), whole_sum(total)

    def exact(picker, values):
        high = values.astype(BF16)
        rest = values - high.astype(F32)
        middle = rest.astype(BF16)
        low = (rest - middle.astype(F32)).astype(BF16)
        return (dot(picker, high, NN) + dot(picker, middle, NN)) + dot(picker, low, NN)

    def both_parts(table, parts):
        parts[0], parts[1] = split(table[...])

    for load in loads[:6]:
        load.wait()
    columns = lax.broadcasted_iota(jnp.int32, (ROWS, NX), 1)
    rows = lax.broadcasted_iota(jnp.int32, (ROWS, NX), 0)
    amp_rows = jnp.sum(
        jnp.where(columns == me * ROWS + rows, col_ref[...], 0.0), axis=1, keepdims=True
    )
    row_ref[...] = jnp.broadcast_to(amp_rows * time_ref[...], (ROWS, 128))
    both_parts(long_ref, long_tab)
    both_parts(edge_ref, edge_tab)
    rows_to_columns(right_ref, 0)
    right_sum = whole_sum(right_ref[...] * right_ref[...])

    for load in loads[8:13]:
        load.wait()
    chosen = lax.broadcasted_iota(jnp.int32, (64, 64), 0) == trow_ref[...]
    picker = chosen.astype(BF16)
    columns = jnp.sum(
        jnp.where(chosen, tcol_ref[...].astype(F32), 0.0), axis=1, keepdims=True
    )
    for index, ref in enumerate((u_ref, v_ref, noise_ref)):
        vis_out[:, index, :] = exact(picker, ref[...])
    vis_out[:, 3, :] = jnp.broadcast_to(columns, (64, 128))

    for load in loads[6:8]:
        load.wait()
    ordered = exact(order_ref[...].astype(BF16), raw_ref[...])
    for c in range(16):
        turned[128 * c : 128 * (c + 1), 0:32] = ordered[:, 128 * c : 128 * (c + 1)].T
    for a in range(16):
        four = jnp.concatenate(
            [turned[pl.ds(4 * a + r, 32, stride=64), 0:32] for r in range(4)], axis=1
        )
        back = four.T
        for r in range(4):
            tile = jnp.concatenate(
                [back[32 * r + 8 * k : 32 * r + 8 * k + 8] for k in range(4)], axis=1
            )
            for hl in range(4):
                lin_ref[hl, 4 * a + r] = tile[2 * hl : 2 * hl + 2]

    pl.semaphore_wait(barrier, len(OFFSETS) + 7)
    send_full(0)
    place = me % 4
    for step in range(1, 4):
        target = (place + step) % 4
        pltpu.make_async_remote_copy(
            src_ref=lin_ref.at[target], dst_ref=lin_in.at[place], send_sem=lin_s, recv_sem=lin_r,
            device_id=(frame, me - place + target), device_id_type=MESH,
        ).start()
    pltpu.make_async_copy(lin_ref.at[place], lin_in.at[place], lin_r).start()
    send_all(vis_out, vis_in, vis_s, vis_r)
    for load in loads[13:]:
        load.wait()
    both_parts(short_ref, short_tab)
    both_parts(shortp_ref, shortp_tab)

    def build(c, carry):
        def pair(index):
            return jnp.concatenate(
                [vis_in[2 * c, index : index + 1], vis_in[2 * c + 1, index : index + 1]], axis=1
            )

        cells = lax.broadcasted_iota(jnp.int32, (128, 256), 0).astype(F32)
        away = (cells - pair(0)) * (8.0 / 128)
        values = jnp.exp(-0.5 * (away * away))
        high, low = split(values)
        kern_u[c, 0:128] = high
        kern_u[c, 128:256] = low
        high, low = split(values.T)
        kern_t[c, :, 0:128] = high
        kern_t[c, :, 128:256] = low
        cells = lax.broadcasted_iota(jnp.int32, (16, 256), 0).astype(F32)
        away = (cells - pair(1)) * (4.0 / 16)
        kern_v[c] = jnp.exp(-0.5 * (away * away))
        return carry

    arrived(lin_in, lin_r)

    def sky_tile(k):
        return jnp.concatenate([lin_in[r, k] for r in range(4)], axis=0)

    for k in range(1, 32):
        sky[8 * (k - 1) : 8 * k, 0:128] = sky_tile(k)
        sky[8 * (k - 1) : 8 * k, 128:256] = sky_tile(64 - k)
    sky[248:256, 0:128] = sky_tile(0)
    sky[256:264, 0:128] = sky_tile(32)
    sky[248:264, 128:256] = jnp.zeros((16, 128), F32)

    columns_to_band(0)
    arrived(vis_in, vis_r)
    lax.fori_loop(0, CHUNKS, build, 0, unroll=2)
    grid, weight_sum = measure(band_to_grid(0), None, True)
    reduce_send(0, 0, pack(right_sum, weight_sum))
    grid_to_band(grid, 1)
    reduce_send(0, 1, reduce_take(0, 0))
    band_to_columns(1, 1)
    reduce_send(0, 2, reduce_take(0, 1))
    harmonic = columns_to_rows(1)
    sums = reduce_take(0, 2)
    norm_zero = unpack(sums, 0)
    step_zero = norm_zero / (norm_zero + unpack(sums, 1))
    square = jnp.zeros((32, 128), F32)
    cross = jnp.zeros((32, 128), F32)
    for a in range(16):
        lanes = slice(128 * a, 128 * (a + 1))
        before = right_ref[:, lanes]
        after = before - step_zero * (before + harmonic[a])
        resid[:, lanes] = after
        square = square + after * after
        cross = cross + after * before

    reduce_send(1, 0, pack(whole_sum(square), whole_sum(cross)))
    rows_to_columns(resid, 2)
    send_full(2)
    reduce_send(1, 1, reduce_take(1, 0))
    columns_to_band(2)
    reduce_send(1, 2, reduce_take(1, 1))
    grid = band_to_grid(2)
    sums = reduce_take(1, 2)
    norm_one = unpack(sums, 0)
    growth = norm_one / norm_zero
    squared = norm_one + 2.0 * growth * unpack(sums, 1) + growth * growth * norm_zero
    grid, weight_sum = measure(grid, growth, False)
    reduce_send(2, 0, pack(weight_sum))
    grid_to_band(grid, 3)
    reduce_send(2, 1, reduce_take(2, 0))
    band_to_columns(3, 3)
    reduce_send(2, 2, reduce_take(2, 1))
    harmonic = columns_to_rows(3)
    sums = reduce_take(2, 2)
    step_one = norm_one / (squared + unpack(sums, 0))
    for a in range(16):
        lanes = slice(128 * a, 128 * (a + 1))
        before = right_ref[:, lanes]
        after = resid[:, lanes]
        direction = after + growth * before
        sol_ref[:, lanes] = step_zero * before + step_one * direction
        res_ref[:, lanes] = after - step_one * (direction + harmonic[a])

    for n in range(4):
        sent(full_out.at[n], 63, full_s.at[n])
        sent(half_out.at[n], 63, half_s.at[n])
    sent(vis_out, 63, vis_s)
    sent(lin_ref, 3, lin_s)
    for index in range(9):
        sent(red_in.at[index], 7, red_s.at[index])


def shards(
    right_side, amp_time, amp_space, lin_sky, tile_row, tile_col, u_frac, v_frac, noise_weight
):
    order = np.zeros((32, 32))
    for row, (kappa, half, left, k2) in enumerate(np.ndindex(4, 2, 2, 2)):
        index = 4 * left + kappa
        k1 = index if half == 0 else 8 if index == 0 else 16 - index
        order[row, 16 * k2 + k1] = 1.0
    long_main, long_edge, long_twist = long_tables()
    short_main, short_twist = short_tables(lane_rows())
    band_main, band_twist = short_tables(lane_band())
    operands = (
        right_side,
        amp_time.reshape(1, 1),
        amp_space.reshape(1, NX),
        lin_sky,
        tile_row,
        tile_col,
        u_frac,
        v_frac,
        noise_weight,
        jnp.asarray(order, F32),
        *(
            jnp.asarray(t)
            for t in (
                long_main, long_edge, long_twist, short_main, band_main, short_twist, band_twist,
            )
        ),
    )
    vmem = pl.BlockSpec(memory_space=pltpu.VMEM)
    dma = pltpu.SemaphoreType.DMA
    outs = pl.pallas_call(
        kernel,
        out_shape=[jax.ShapeDtypeStruct((ROWS, NX), F32)] * 2,
        in_specs=[pl.BlockSpec(memory_space=pltpu.MemorySpace.HBM)] * len(operands),
        out_specs=[vmem] * 2,
        scratch_shapes=[
            pltpu.VMEM((ROWS, NX), F32),
            *(pltpu.VMEM(o.shape, o.dtype) for o in operands[1:3]),
            pltpu.VMEM((ROWS, NX), F32),
            *(pltpu.VMEM(o.shape, o.dtype) for o in operands[4:6]),
            *[pltpu.VMEM((BLOCKS, 128), F32)] * 3,
            *(pltpu.VMEM(o.shape, o.dtype) for o in operands[9:]),
            *[pltpu.VMEM((2, 256, 256), BF16)] * 4,
            pltpu.VMEM((ROWS, 128), F32),
            pltpu.VMEM((NX, 128), F32),
            pltpu.VMEM((4, 64, 2, 128), F32),
            pltpu.VMEM((4, 64, 8, 128), F32),
            pltpu.VMEM((4, 64, 8, 128), F32),
            pltpu.VMEM((4, 64, 4, 128), F32),
            pltpu.VMEM((4, 64, 4, 128), F32),
            pltpu.VMEM((64, 4, 128), F32),
            pltpu.VMEM((64, 4, 128), F32),
            pltpu.VMEM((4, 64, 2, 128), F32),
            pltpu.VMEM((9, 8, 128), F32),
            pltpu.VMEM((9, 7, 8, 128), F32),
            pltpu.VMEM((CHUNKS, 256, 256), BF16),
            pltpu.VMEM((CHUNKS, 256, 256), BF16),
            pltpu.VMEM((CHUNKS, BAND, 256), F32),
            pltpu.VMEM((264, 256), F32),
            pltpu.VMEM((264, 256), F32),
            pltpu.VMEM((CHUNKS, 8, 256), F32),
            pltpu.VMEM((ROWS, NX), F32),
            dma((4,)), dma((4,)), dma((4,)), dma((4,)),
            dma, dma, dma, dma,
            dma((9,)), dma((9,)), dma((17,)),
        ],
        compiler_params=pltpu.CompilerParams(
            collective_id=0, has_side_effects=True, vmem_limit_bytes=63 * 1024 * 1024
        ),
    )(*operands)
    return tuple(out.reshape(1, ROWS, NX) for out in outs)


def solution(mesh):
    in_specs = (
        P("tm", "space", None),
        P("tm"),
        P(),
        P("space", "tm", None),
        P("tm", "space"),
        P("tm", "space"),
        P("tm", "space", None),
        P("tm", "space", None),
        P("tm", "space", None),
    )
    out_specs = (P("tm", "space", None), P("tm", "space", None))
    return jax.shard_map(shards, mesh=mesh, in_specs=in_specs, out_specs=out_specs, check_vma=False)
```
